256 devices in a mesh: group: 8 (over z), member: 32 (over y, x, core).
Axes of the slice: x: 4, y: 4, z: 8, core: 2. Of those that a mesh axis runs over, the one named last changes fastest.
Arguments:
- embeddings: bfloat16 [196608, 1024], P(('group', 'member')), may hold values from -18 to 18
- prior: float32 [196608, 1000], P(('group', 'member')), may hold values from 0.05 to 5
- source_member: int32 [8, 32, 4], P('group'), may hold values from 0 to 31, as said below
- source_block: int32 [8, 32, 4], P('group'), may hold values from 0 to 5
- cross_block: int32 [8, 32, 2], P(None, 'member'), may hold values from 0 to 5
- row_links: int32 [196608, 4], P(('group', 'member')), may hold values from 0 to 5
Outputs:
- propagated: float32 [196608, 1000], P(('group', 'member'))
The draws below stay inside these ranges and needn't reach their ends.
Inputs may be any that keep to these rules, and one draw needn't show every extreme that they name: `source_member`: no device names itself, and the members in one device's list are distinct. Over all lists of one group no member is named more than 7 times, and in every group some member is named exactly 7 times.
All inputs are finite; a program needn't handle non-finite values.
Results may differ from the reference program's by a relative error of at most 0.0079.
Values may be sent and summed in bfloat16 or wider, within the bound.
No kernel may reach another device: no remote copies, remote signals or barrier semaphores. Data moves between devices by JAX's collectives and lax.ppermute only.
A program may use at most 64 MiB of HBM per device.

```python
import math
import jax
import jax.numpy as jnp
from jax import lax

D = 1024
C = 1000
ROWS_DEV = 768
BR = 128
IN_SLOTS = 4
CROSS = 2
SERVE_CAP = 7
LINKS = 4
ITERS = 2
BLOCKS_DEV = 6
SLOTS = 6
TOTAL = 196608
N_GROUP = 8
N_MEMBER = 32


def link_table(key):
    return jax.random.randint(jax.random.fold_in(key, 31), (TOTAL, LINKS), 0, SLOTS).astype(jnp.int32)


def draw_row_links(key, part):
    return link_table(key)


def draw_embeddings(key, part):
    return jnp.clip(jax.random.normal(key, (TOTAL, D), jnp.float32), -6.0, 6.0).astype(jnp.bfloat16)


def arranged(subkey):
    order = jax.random.permutation(subkey, N_MEMBER).astype(jnp.int32)
    positions = jnp.arange(N_MEMBER, dtype=jnp.int32)
    offsets = jnp.arange(1, IN_SLOTS + 1, dtype=jnp.int32)
    at_position = order[(positions[:, None] + offsets[None, :]) % N_MEMBER]
    redirect = (positions[:, None] >= 1) & (positions[:, None] <= SERVE_CAP - IN_SLOTS) & (offsets[None, :] == 1)
    at_position = jnp.where(redirect, order[0], at_position)
    return jnp.zeros((N_MEMBER, IN_SLOTS), jnp.int32).at[order].set(at_position)


def draw_source_member(key, part):
    subkeys = jax.random.split(jax.random.fold_in(key, 21), N_GROUP)
    return jax.vmap(arranged)(subkeys).astype(jnp.int32)


def place_ends(values, stream_key, smallest, largest):
    extent = values.shape
    place = [jax.random.randint(jax.random.fold_in(stream_key, axis), (), 0, extent[axis]) for axis in range(len(extent))]
    values = values.at[tuple(place)].set(smallest)
    longest = extent.index(max(extent))
    place[longest] = (place[longest] + 1) % extent[longest]
    return values.at[tuple(place)].set(largest)


def steps_of(rng, dims, cuts, least, largest):
    factor_of = 1.0
    for axis_at, blocks in cuts:
        draws = jax.random.uniform(jax.random.fold_in(jax.random.fold_in(rng, 6), axis_at), (blocks,), jnp.float32, least / len(cuts), largest / len(cuts))
        factor_of = factor_of * jnp.repeat(jnp.exp(draws), dims[axis_at] // blocks).reshape((-1,) + (1,) * (len(dims) - 1 - axis_at))
    return factor_of


def setup_inputs(seed: int = 0) -> dict:
    streams_of = jax.random.split(jax.random.key(seed), 7)
    return {
        "embeddings": draw_embeddings(jax.random.fold_in(streams_of[6], 71), 0),
        "prior": jnp.clip(jnp.exp(math.log(5.0) - 4.6051702 * jax.random.uniform(streams_of[1], (TOTAL, C), jnp.float32) ** steps_of(streams_of[1], (TOTAL, C), ((0, 256),), -0.2, 0.2)), 0.05, 5.0),
        "source_member": draw_source_member(jax.random.fold_in(streams_of[6], 71), 0),
        "source_block": place_ends(jax.random.randint(streams_of[3], (N_GROUP, N_MEMBER, IN_SLOTS), 0, BLOCKS_DEV), jax.random.fold_in(streams_of[3], 1), 0, BLOCKS_DEV - 1).astype(jnp.int32),
        "cross_block": place_ends(jax.random.randint(streams_of[4], (N_GROUP, N_MEMBER, CROSS), 0, BLOCKS_DEV), jax.random.fold_in(streams_of[4], 1), 0, BLOCKS_DEV - 1).astype(jnp.int32),
        "row_links": draw_row_links(jax.random.fold_in(streams_of[6], 71), 0),
    }


MIXING = 0.8


def allowed_mask(row_links):
    slot_ids = jnp.arange(SLOTS, dtype=jnp.int32)
    slot_hits = jnp.any(row_links[:, :, None] == slot_ids[None, None, :], axis=1)
    neighbour_mask = jnp.repeat(slot_hits, BR, axis=1)
    local_mask = jnp.logical_not(jnp.eye(ROWS_DEV, dtype=bool))
    return jnp.concatenate([local_mask, neighbour_mask], axis=1)


def kernel_weights(queries, key_rows, allowed):
    scores = jnp.dot(queries, key_rows.T, preferred_element_type=jnp.float32) * (D ** -0.5)
    scores = jnp.where(allowed, scores, -jnp.inf)
    highest = jnp.max(scores, axis=1, keepdims=True)
    powers = jnp.where(allowed, jnp.exp(scores - highest), 0.0)
    return (powers / jnp.sum(powers, axis=1, keepdims=True)).astype(jnp.bfloat16)


def sharpen(weights, key_labels, prior_share):
    mixed = MIXING * jnp.dot(weights, key_labels, preferred_element_type=jnp.float32) + (1.0 - MIXING) * prior_share
    squared = mixed * mixed
    return squared / jnp.sum(squared, axis=1, keepdims=True)


def collect(blocks_all, device, members, block_ids, cross_ids):
    group_index = device // N_MEMBER
    member_index = device % N_MEMBER
    inner = blocks_all[group_index * N_MEMBER + members, block_ids]
    below_device = ((group_index + N_GROUP - 1) % N_GROUP) * N_MEMBER + member_index
    above_device = ((group_index + 1) % N_GROUP) * N_MEMBER + member_index
    outer = blocks_all[jnp.stack([below_device, above_device]).astype(jnp.int32), cross_ids]
    lane_count = blocks_all.shape[-1]
    return jnp.concatenate([inner.reshape(-1, lane_count), outer.reshape(-1, lane_count)], axis=0)


def reference(embeddings, prior, source_member, source_block, cross_block, row_links):
    devices = N_GROUP * N_MEMBER
    emb_blocks = embeddings.reshape(devices, ROWS_DEV // BR, BR, D)
    prior_share = prior / jnp.sum(prior, axis=1, keepdims=True)
    labels = prior_share.astype(jnp.bfloat16)
    device_ids = jnp.arange(devices, dtype=jnp.int32)
    emb_dev = embeddings.reshape(devices, ROWS_DEV, D)
    share_dev = prior_share.reshape(devices, ROWS_DEV, C)
    links_dev = row_links.reshape(devices, ROWS_DEV, LINKS)
    members_dev = source_member.reshape(devices, IN_SLOTS)
    blocks_dev = source_block.reshape(devices, IN_SLOTS)
    cross_dev = cross_block.reshape(devices, CROSS)
    result = prior_share
    for iteration in range(ITERS):
        lab_blocks = labels.reshape(devices, ROWS_DEV // BR, BR, C)
        lab_dev = labels.reshape(devices, ROWS_DEV, C)

        def one_device(items):
            device, queries, own_labels, share_rows, links, members, block_ids, cross_ids = items
            key_rows = jnp.concatenate([queries, collect(emb_blocks, device, members, block_ids, cross_ids)], axis=0)
            key_labels = jnp.concatenate([own_labels, collect(lab_blocks, device, members, block_ids, cross_ids)], axis=0)
            weights = kernel_weights(queries, key_rows, allowed_mask(links))
            return sharpen(weights, key_labels, share_rows)

        result = lax.map(one_device, (device_ids, emb_dev, lab_dev, share_dev, links_dev, members_dev, blocks_dev, cross_dev))
        result = result.reshape(devices * ROWS_DEV, C)
        labels = result.astype(jnp.bfloat16)
    return result * C
```

```python
import jax
import jax.numpy as jnp
from jax import lax
from jax.experimental import pallas as pl
from jax.experimental.pallas import tpu as pltpu
from jax.sharding import PartitionSpec as P

BR = 128
MIXING = 0.8
SUB = 32
QB = 256
BF = jnp.bfloat16
F32 = jnp.float32
VMEM_BYTES = 24 * 1024 * 1024


def params():
    return pltpu.CompilerParams(
        dimension_semantics=("arbitrary",), vmem_limit_bytes=VMEM_BYTES
    )


def cost(flops, size, exps=0):
    return pl.CostEstimate(flops=flops, bytes_accessed=size, transcendentals=exps)


def nt(a, b):
    return lax.dot_general(a, b, (((1,), (1,)), ((), ())), preferred_element_type=F32)


def nn(a, b):
    return jnp.dot(a, b, preferred_element_type=F32)


def padded(x, rows):
    return jnp.concatenate([x, jnp.zeros((rows - x.shape[0], x.shape[1]), x.dtype)], axis=0)


def share_of(prior_ref):
    prior = prior_ref[...]
    return prior / jnp.sum(prior, axis=0, keepdims=True)


def prep_kernel(prior_ref, emb_ref, out_ref):
    relays = out_ref.shape[0]
    labels = padded(share_of(prior_ref), relays * SUB).astype(BF)
    out_ref[:, :SUB, :] = labels.reshape(relays, SUB, BR)
    wide = emb_ref.shape[1] // BR
    for r in range(BR // SUB):
        for f in range(wide):
            out_ref[r * wide + f, SUB:, :] = emb_ref[r * SUB : (r + 1) * SUB, f * BR : (f + 1) * BR]


def prep(prior_t, emb, relays):
    classes, rows = prior_t.shape
    features = emb.shape[1]
    return pl.pallas_call(
        prep_kernel,
        grid=(rows // BR,),
        in_specs=[
            pl.BlockSpec((classes, BR), lambda i: (0, i)),
            pl.BlockSpec((BR, features), lambda i: (i, 0)),
        ],
        out_specs=pl.BlockSpec((relays, 2 * SUB, BR), lambda i: (0, 0, i)),
        out_shape=jax.ShapeDtypeStruct((relays, 2 * SUB, rows), BF),
        compiler_params=params(),
        cost_estimate=cost(4 * classes * rows, 4 * classes * rows + 4 * features * rows),
        name="prep",
    )(prior_t, emb)


def select_kernel(owner_ref, block_ref, got_ref, out_ref):
    members, slots = owner_ref.shape

    @pl.loop(0, members)
    def _(d):
        for k in range(slots):
            lane = pl.multiple_of(block_ref[d, k] * BR, BR)
            out_ref[d, :, k * BR : (k + 1) * BR] = got_ref[owner_ref[d, k], :, pl.ds(lane, BR)]


def select(owners, blocks, got):
    members, slots = owners.shape
    depth = got.shape[1]
    return pl.pallas_call(
        select_kernel,
        in_specs=[
            pl.BlockSpec(memory_space=pltpu.SMEM),
            pl.BlockSpec(memory_space=pltpu.SMEM),
            pl.BlockSpec(memory_space=pltpu.VMEM),
        ],
        out_specs=pl.BlockSpec(memory_space=pltpu.VMEM),
        out_shape=jax.ShapeDtypeStruct((members, depth, slots * BR), BF),
        compiler_params=pltpu.CompilerParams(vmem_limit_bytes=VMEM_BYTES),
        cost_estimate=cost(0, 4 * got.size),
        name="select",
    )(owners, blocks, got)


def pack_kernel(pick_ref, emb_ref, lab_ref, out_ref):
    out_ref[:BR] = emb_ref[...]
    labels = lab_ref[...].reshape(-1, BR)
    for f in range(labels.shape[0] // BR):
        out_ref[BR:, f * BR : (f + 1) * BR] = labels[f * BR : (f + 1) * BR]


def pack(pick, emb, spread):
    relays = spread.shape[0]
    features = emb.shape[1]
    return pl.pallas_call(
        pack_kernel,
        grid_spec=pltpu.PrefetchScalarGridSpec(
            num_scalar_prefetch=1,
            grid=(1,),
            in_specs=[
                pl.BlockSpec((BR, features), lambda i, p: (p[0], 0)),
                pl.BlockSpec((relays, SUB, BR), lambda i, p: (0, 0, p[0])),
            ],
            out_specs=pl.BlockSpec((2 * BR, features), lambda i, p: (0, 0)),
        ),
        out_shape=jax.ShapeDtypeStruct((2 * BR, features), BF),
        compiler_params=params(),
        cost_estimate=cost(0, 8 * BR * features),
        name="pack_cross",
    )(pick, emb, spread)


def pack_labels_kernel(pick_ref, lab_ref, out_ref):
    out_ref[...] = lab_ref[...]


def pack_labels(pick, labels_t):
    depth = labels_t.shape[0]
    return pl.pallas_call(
        pack_labels_kernel,
        grid_spec=pltpu.PrefetchScalarGridSpec(
            num_scalar_prefetch=1,
            grid=(1,),
            in_specs=[pl.BlockSpec((depth, BR), lambda i, p: (0, p[0]))],
            out_specs=pl.BlockSpec((depth, BR), lambda i, p: (0, 0)),
        ),
        out_shape=jax.ShapeDtypeStruct((depth, BR), BF),
        compiler_params=params(),
        cost_estimate=cost(0, 4 * BR * depth),
        name="pack_labels",
    )(pick, labels_t)


def slot_hit(links, slot):
    return jnp.max(jnp.where(links == slot, 1.0, 0.0), axis=0, keepdims=True) > 0.0


def own_kernel(near_slots, emb_ref, q_ref, lab_ref, below_ref, above_ref, links_ref, p_ref, mix_ref, stat_ref, far_ref):
    step = pl.program_id(0)
    rows, features = emb_ref.shape
    depth = mix_ref.shape[0]

    @pl.when(step == 0)
    def _():
        for f in range(depth // BR):
            for s, ref in enumerate((below_ref, above_ref)):
                far_ref[f * BR : (f + 1) * BR, s * BR : (s + 1) * BR] = ref[BR:, f * BR : (f + 1) * BR]

    q = q_ref[...]
    scale = features ** (-0.5)
    own = nt(emb_ref[...], q) * scale
    key_id = lax.broadcasted_iota(jnp.int32, own.shape, 0)
    row_id = lax.broadcasted_iota(jnp.int32, own.shape, 1) + step * QB
    own = jnp.where(key_id == row_id, -jnp.inf, own)
    links = links_ref[...]
    parts = [own]
    for s, ref in enumerate((below_ref, above_ref)):
        far = nt(ref[:BR], q) * scale
        parts.append(jnp.where(slot_hit(links, near_slots + s), far, -jnp.inf))
    scores = jnp.concatenate(parts, axis=0)
    top = jnp.max(scores, axis=0, keepdims=True)
    powers = jnp.exp(scores - top)
    total = jnp.sum(powers, axis=0, keepdims=True)
    powers = powers.astype(BF)
    p_ref[...] = powers
    mix_ref[...] = nn(lab_ref[...].reshape(depth, rows), powers[:rows]) + nn(far_ref[...], powers[rows:])
    stat_ref[...] = jnp.concatenate([top, total, jnp.zeros((6, QB), F32)], axis=0)


def own_part(emb, spread, below, above, links_t, near_slots):
    rows, features = emb.shape
    relays = spread.shape[0]
    depth = relays * SUB
    keys = rows + 2 * BR
    return pl.pallas_call(
        lambda *refs: own_kernel(near_slots, *refs),
        grid=(rows // QB,),
        in_specs=[
            pl.BlockSpec((rows, features), lambda i: (0, 0)),
            pl.BlockSpec((QB, features), lambda i: (i, 0)),
            pl.BlockSpec((relays, SUB, rows), lambda i: (0, 0, 0)),
            pl.BlockSpec((2 * BR, features), lambda i: (0, 0)),
            pl.BlockSpec((2 * BR, features), lambda i: (0, 0)),
            pl.BlockSpec((links_t.shape[0], QB), lambda i: (0, i)),
        ],
        out_specs=[
            pl.BlockSpec((keys, QB), lambda i: (0, i)),
            pl.BlockSpec((depth, QB), lambda i: (0, i)),
            pl.BlockSpec((8, QB), lambda i: (0, i)),
        ],
        out_shape=[
            jax.ShapeDtypeStruct((keys, rows), BF),
            jax.ShapeDtypeStruct((depth, rows), F32),
            jax.ShapeDtypeStruct((8, rows), F32),
        ],
        scratch_shapes=[pltpu.VMEM((depth, 2 * BR), BF)],
        compiler_params=params(),
        cost_estimate=cost(4 * keys * rows * features, 12 * depth * rows, keys * rows),
        name="own_part",
    )(emb, emb, spread, below, above, links_t)


def near_kernel(got_ref, q_ref, links_ref, mix_ref, stat_ref, prior_ref, lab_ref, p_ref, out_ref, key_ref):
    step = pl.program_id(0)
    features = q_ref.shape[1]
    relays = got_ref.shape[0]
    slots = got_ref.shape[2] // BR
    wide = features // BR

    @pl.when(step == 0)
    def _():
        for s in range(slots):
            for r in range(BR // SUB):
                at = s * BR + r * SUB
                for f in range(wide):
                    key_ref[at : at + SUB, f * BR : (f + 1) * BR] = got_ref[
                        r * wide + f, SUB:, s * BR : (s + 1) * BR
                    ]

    links = links_ref[...]
    scores = nt(key_ref[...], q_ref[...]) * features ** (-0.5)
    scores = jnp.concatenate(
        [
            jnp.where(slot_hit(links, s), scores[s * BR : (s + 1) * BR], -jnp.inf)
            for s in range(slots)
        ],
        axis=0,
    )
    own_top = stat_ref[0:1]
    top = jnp.maximum(own_top, jnp.max(scores, axis=0, keepdims=True))
    powers = jnp.exp(scores - top)
    lower = jnp.exp(own_top - top)
    inverse = MIXING / (lower * stat_ref[1:2] + jnp.sum(powers, axis=0, keepdims=True))
    lower = lower * inverse
    powers = powers.astype(BF)
    p_ref[...] = powers
    out_ref[...] = jnp.concatenate([lower, inverse, jnp.zeros((6, QB), F32)], axis=0)
    near = nn(got_ref[:, :SUB, :].reshape(relays * SUB, slots * BR), powers)
    sharp = sharpened(mix_ref[...] * lower + near * inverse, prior_ref)
    lab_ref[...] = padded(sharp, relays * SUB).astype(BF)


def sharpened(mixed, prior_ref):
    share = share_of(prior_ref)
    mixed = mixed[: share.shape[0]] + (1.0 - MIXING) * share
    squared = mixed * mixed
    return squared / jnp.sum(squared, axis=0, keepdims=True)


def near_part(got, emb, links_t, mix, stat, prior_t):
    rows, features = emb.shape
    relays, depth2, near_keys = got.shape
    classes = prior_t.shape[0]
    depth = relays * SUB
    return pl.pallas_call(
        near_kernel,
        grid=(rows // QB,),
        in_specs=[
            pl.BlockSpec((relays, depth2, near_keys), lambda i: (0, 0, 0)),
            pl.BlockSpec((QB, features), lambda i: (i, 0)),
            pl.BlockSpec((links_t.shape[0], QB), lambda i: (0, i)),
            pl.BlockSpec((depth, QB), lambda i: (0, i)),
            pl.BlockSpec((8, QB), lambda i: (0, i)),
            pl.BlockSpec((classes, QB), lambda i: (0, i)),
        ],
        out_specs=[
            pl.BlockSpec((depth, QB), lambda i: (0, i)),
            pl.BlockSpec((near_keys, QB), lambda i: (0, i)),
            pl.BlockSpec((8, QB), lambda i: (0, i)),
        ],
        out_shape=[
            jax.ShapeDtypeStruct((depth, rows), BF),
            jax.ShapeDtypeStruct((near_keys, rows), BF),
            jax.ShapeDtypeStruct((8, rows), F32),
        ],
        scratch_shapes=[pltpu.VMEM((near_keys, features), BF)],
        compiler_params=params(),
        cost_estimate=cost(4 * near_keys * rows * features, 12 * depth * rows, near_keys * rows),
        name="near_part",
    )(got, emb, links_t, mix, stat, prior_t)


def remix_kernel(lab_ref, below_ref, above_ref, p_ref, out_ref):
    rows = lab_ref.shape[1]
    far = jnp.concatenate([below_ref[...], above_ref[...]], axis=1)
    out_ref[...] = nn(lab_ref[...], p_ref[:rows]) + nn(far, p_ref[rows:])


def remix(labels_t, below, above, powers):
    depth, rows = labels_t.shape
    keys = powers.shape[0]
    return pl.pallas_call(
        remix_kernel,
        grid=(rows // QB,),
        in_specs=[
            pl.BlockSpec((depth, rows), lambda i: (0, 0)),
            pl.BlockSpec((depth, BR), lambda i: (0, 0)),
            pl.BlockSpec((depth, BR), lambda i: (0, 0)),
            pl.BlockSpec((keys, QB), lambda i: (0, i)),
        ],
        out_specs=pl.BlockSpec((depth, QB), lambda i: (0, i)),
        out_shape=jax.ShapeDtypeStruct((depth, rows), F32),
        compiler_params=params(),
        cost_estimate=cost(2 * keys * rows * depth, 8 * depth * rows),
        name="remix",
    )(labels_t, below, above, powers)


def last_kernel(got_ref, p_ref, mix_ref, scale_ref, prior_ref, out_ref):
    relays, sub, near_keys = got_ref.shape
    near = nn(got_ref[...].reshape(relays * sub, near_keys), p_ref[...])
    mixed = mix_ref[...] * scale_ref[0:1] + near * scale_ref[1:2]
    sharp = sharpened(mixed, prior_ref)
    out_ref[...] = sharp * float(out_ref.shape[0])


def last_part(got, powers, mix, scales, prior_t):
    relays, sub, near_keys = got.shape
    classes, rows = prior_t.shape
    depth = relays * sub
    return pl.pallas_call(
        last_kernel,
        grid=(rows // QB,),
        in_specs=[
            pl.BlockSpec((relays, sub, near_keys), lambda i: (0, 0, 0)),
            pl.BlockSpec((near_keys, QB), lambda i: (0, i)),
            pl.BlockSpec((depth, QB), lambda i: (0, i)),
            pl.BlockSpec((8, QB), lambda i: (0, i)),
            pl.BlockSpec((classes, QB), lambda i: (0, i)),
        ],
        out_specs=pl.BlockSpec((classes, QB), lambda i: (0, i)),
        out_shape=jax.ShapeDtypeStruct((classes, rows), F32),
        compiler_params=params(),
        cost_estimate=cost(2 * near_keys * rows * depth, 12 * depth * rows),
        name="last_part",
    )(got, powers, mix, scales, prior_t)


def exchanged(x):
    return lax.all_to_all(x, "member", split_axis=0, concat_axis=0, tiled=True)


def body(embeddings, prior, source_member, source_block, cross_block, row_links):
    relays = lax.axis_size("member")
    groups = lax.axis_size("group")
    group = lax.axis_index("group")
    rows = embeddings.shape[0]
    owners, blocks = source_member[0], source_block[0]
    near_slots = owners.shape[1]
    prior_t, links_t = prior.T, row_links.T
    up = [(i, (i + 1) % groups) for i in range(groups)]
    down = [(j, i) for i, j in up]
    asked = cross_block[:, 0, :]
    to_above = lax.dynamic_slice(asked, ((group + 1) % groups, 0), (1, 1)).reshape(1)
    to_below = lax.dynamic_slice(asked, ((group + groups - 1) % groups, 1), (1, 1)).reshape(1)

    spread = prep(prior_t, embeddings, relays)
    relayed = exchanged(spread)
    below = lax.ppermute(pack(to_above, embeddings, spread), "group", up)
    above = lax.ppermute(pack(to_below, embeddings, spread), "group", down)
    far_powers, mix, stat = own_part(embeddings, spread, below, above, links_t, near_slots)
    near = exchanged(select(owners, blocks, relayed))
    labels_t, near_powers, scales = near_part(near, embeddings, links_t, mix, stat, prior_t)

    relayed = exchanged(labels_t.reshape(relays, SUB, rows))
    below = lax.ppermute(pack_labels(to_above, labels_t), "group", up)
    above = lax.ppermute(pack_labels(to_below, labels_t), "group", down)
    mix = remix(labels_t, below, above, far_powers)
    near = exchanged(select(owners, blocks, relayed))
    return last_part(near, near_powers, mix, scales, prior_t).T


def solution(mesh):
    placed = (
        P(("group", "member"), None),
        P(("group", "member"), None),
        P("group", None, None),
        P("group", None, None),
        P(None, "member", None),
        P(("group", "member"), None),
    )
    return jax.shard_map(
        body, mesh=mesh, in_specs=placed, out_specs=P(("group", "member"), None), check_vma=False
    )
```

```python
import jax
import jax.numpy as jnp
from jax import lax
from jax.experimental import pallas as pl
from jax.experimental.pallas import tpu as pltpu
from jax.sharding import PartitionSpec as P

BR = 128
MIXING = 0.8
SUB = 32
QB = 256
BF = jnp.bfloat16
F32 = jnp.float32
VMEM_BYTES = 24 * 1024 * 1024


def params():
    return pltpu.CompilerParams(
        dimension_semantics=("arbitrary",), vmem_limit_bytes=VMEM_BYTES
    )


def in_hbm(x):
    return pltpu.with_memory_space_constraint(x, pltpu.HBM)


def cost(flops, size, exps=0):
    return pl.CostEstimate(flops=flops, bytes_accessed=size, transcendentals=exps)


def nt(a, b):
    return lax.dot_general(a, b, (((1,), (1,)), ((), ())), preferred_element_type=F32)


def nn(a, b):
    return jnp.dot(a, b, preferred_element_type=F32)


def padded(x, rows):
    return jnp.concatenate([x, jnp.zeros((rows - x.shape[0], x.shape[1]), x.dtype)], axis=0)


def share_of(prior_ref):
    prior = prior_ref[...]
    return prior / jnp.sum(prior, axis=0, keepdims=True)


def prep_kernel(prior_ref, emb_ref, out_ref):
    relays = out_ref.shape[0]
    labels = padded(share_of(prior_ref), relays * SUB).astype(BF)
    out_ref[:, :SUB, :] = labels.reshape(relays, SUB, BR)
    wide = emb_ref.shape[1] // BR
    for r in range(BR // SUB):
        for f in range(wide):
            out_ref[r * wide + f, SUB:, :] = emb_ref[r * SUB : (r + 1) * SUB, f * BR : (f + 1) * BR]


def prep(prior_t, emb, relays):
    classes, rows = prior_t.shape
    features = emb.shape[1]
    return pl.pallas_call(
        prep_kernel,
        grid=(rows // BR,),
        in_specs=[
            pl.BlockSpec((classes, BR), lambda i: (0, i)),
            pl.BlockSpec((BR, features), lambda i: (i, 0)),
        ],
        out_specs=pl.BlockSpec((relays, 2 * SUB, BR), lambda i: (0, 0, i)),
        out_shape=jax.ShapeDtypeStruct((relays, 2 * SUB, rows), BF),
        compiler_params=params(),
        cost_estimate=cost(4 * classes * rows, 4 * classes * rows + 4 * features * rows),
        name="prep",
    )(in_hbm(prior_t), in_hbm(emb))


def select_kernel(owner_ref, block_ref, got_ref, after_ref, out_ref):
    members, slots = owner_ref.shape

    @pl.loop(0, members)
    def _(d):
        for k in range(slots):
            lane = pl.multiple_of(block_ref[d, k] * BR, BR)
            out_ref[d, :, k * BR : (k + 1) * BR] = got_ref[owner_ref[d, k], :, pl.ds(lane, BR)]


def select(owners, blocks, got, after):
    members, slots = owners.shape
    depth = got.shape[1]
    return pl.pallas_call(
        select_kernel,
        in_specs=[
            pl.BlockSpec(memory_space=pltpu.SMEM),
            pl.BlockSpec(memory_space=pltpu.SMEM),
            pl.BlockSpec(memory_space=pltpu.VMEM),
            pl.BlockSpec(memory_space=pl.ANY),
        ],
        out_specs=pl.BlockSpec(memory_space=pltpu.VMEM),
        out_shape=jax.ShapeDtypeStruct((members, depth, slots * BR), BF),
        compiler_params=pltpu.CompilerParams(vmem_limit_bytes=VMEM_BYTES),
        cost_estimate=cost(0, 4 * got.size),
        name="select",
    )(owners, blocks, got, after)


def pack_kernel(pick_ref, emb_ref, lab_ref, out_ref):
    out_ref[:BR] = emb_ref[...]
    labels = lab_ref[...].reshape(-1, BR)
    for f in range(labels.shape[0] // BR):
        out_ref[BR:, f * BR : (f + 1) * BR] = labels[f * BR : (f + 1) * BR]


def pack(pick, emb, spread):
    relays = spread.shape[0]
    features = emb.shape[1]
    return pl.pallas_call(
        pack_kernel,
        grid_spec=pltpu.PrefetchScalarGridSpec(
            num_scalar_prefetch=1,
            grid=(1,),
            in_specs=[
                pl.BlockSpec((BR, features), lambda i, p: (p[0], 0)),
                pl.BlockSpec((relays, SUB, BR), lambda i, p: (0, 0, p[0])),
            ],
            out_specs=pl.BlockSpec((2 * BR, features), lambda i, p: (0, 0)),
        ),
        out_shape=jax.ShapeDtypeStruct((2 * BR, features), BF),
        compiler_params=params(),
        cost_estimate=cost(0, 8 * BR * features),
        name="pack_cross",
    )(pick, emb, spread)


def pack_labels_kernel(pick_ref, lab_ref, out_ref):
    out_ref[...] = lab_ref[...]


def pack_labels(pick, labels_t):
    depth = labels_t.shape[0]
    return pl.pallas_call(
        pack_labels_kernel,
        grid_spec=pltpu.PrefetchScalarGridSpec(
            num_scalar_prefetch=1,
            grid=(1,),
            in_specs=[pl.BlockSpec((depth, BR), lambda i, p: (0, p[0]))],
            out_specs=pl.BlockSpec((depth, BR), lambda i, p: (0, 0)),
        ),
        out_shape=jax.ShapeDtypeStruct((depth, BR), BF),
        compiler_params=params(),
        cost_estimate=cost(0, 4 * BR * depth),
        name="pack_labels",
    )(pick, labels_t)


def slot_hit(links, slot):
    return jnp.max(jnp.where(links == slot, 1.0, 0.0), axis=0, keepdims=True) > 0.0


def own_kernel(near_slots, emb_ref, q_ref, lab_ref, below_ref, above_ref, links_ref, p_ref, mix_ref, stat_ref, far_ref):
    step = pl.program_id(0)
    rows, features = emb_ref.shape
    depth = mix_ref.shape[0]

    @pl.when(step == 0)
    def _():
        for f in range(depth // BR):
            for s, ref in enumerate((below_ref, above_ref)):
                far_ref[f * BR : (f + 1) * BR, s * BR : (s + 1) * BR] = ref[BR:, f * BR : (f + 1) * BR]

    q = q_ref[...]
    scale = features ** (-0.5)
    own = nt(emb_ref[...], q) * scale
    key_id = lax.broadcasted_iota(jnp.int32, own.shape, 0)
    row_id = lax.broadcasted_iota(jnp.int32, own.shape, 1) + step * QB
    own = jnp.where(key_id == row_id, -jnp.inf, own)
    links = links_ref[...]
    parts = [own]
    for s, ref in enumerate((below_ref, above_ref)):
        far = nt(ref[:BR], q) * scale
        parts.append(jnp.where(slot_hit(links, near_slots + s), far, -jnp.inf))
    scores = jnp.concatenate(parts, axis=0)
    top = jnp.max(scores, axis=0, keepdims=True)
    powers = jnp.exp(scores - top)
    total = jnp.sum(powers, axis=0, keepdims=True)
    powers = powers.astype(BF)
    p_ref[...] = powers
    mix_ref[...] = nn(lab_ref[...].reshape(depth, rows), powers[:rows]) + nn(far_ref[...], powers[rows:])
    stat_ref[...] = jnp.concatenate([top, total, jnp.zeros((6, QB), F32)], axis=0)


def own_part(emb, spread, below, above, links_t, near_slots):
    rows, features = emb.shape
    relays = spread.shape[0]
    depth = relays * SUB
    keys = rows + 2 * BR
    return pl.pallas_call(
        lambda *refs: own_kernel(near_slots, *refs),
        grid=(rows // QB,),
        in_specs=[
            pl.BlockSpec((rows, features), lambda i: (0, 0)),
            pl.BlockSpec((QB, features), lambda i: (i, 0)),
            pl.BlockSpec((relays, SUB, rows), lambda i: (0, 0, 0)),
            pl.BlockSpec((2 * BR, features), lambda i: (0, 0)),
            pl.BlockSpec((2 * BR, features), lambda i: (0, 0)),
            pl.BlockSpec((links_t.shape[0], QB), lambda i: (0, i)),
        ],
        out_specs=[
            pl.BlockSpec((keys, QB), lambda i: (0, i)),
            pl.BlockSpec((depth, QB), lambda i: (0, i)),
            pl.BlockSpec((8, QB), lambda i: (0, i)),
        ],
        out_shape=[
            jax.ShapeDtypeStruct((keys, rows), BF),
            jax.ShapeDtypeStruct((depth, rows), F32),
            jax.ShapeDtypeStruct((8, rows), F32),
        ],
        scratch_shapes=[pltpu.VMEM((depth, 2 * BR), BF)],
        compiler_params=params(),
        cost_estimate=cost(4 * keys * rows * features, 12 * depth * rows, keys * rows),
        name="own_part",
    )(emb, emb, spread, below, above, links_t)


def near_kernel(got_ref, q_ref, links_ref, mix_ref, stat_ref, prior_ref, lab_ref, p_ref, out_ref, key_ref):
    step = pl.program_id(0)
    features = q_ref.shape[1]
    relays = got_ref.shape[0]
    slots = got_ref.shape[2] // BR
    wide = features // BR

    @pl.when(step == 0)
    def _():
        for s in range(slots):
            for r in range(BR // SUB):
                at = s * BR + r * SUB
                for f in range(wide):
                    key_ref[at : at + SUB, f * BR : (f + 1) * BR] = got_ref[
                        r * wide + f, SUB:, s * BR : (s + 1) * BR
                    ]

    links = links_ref[...]
    scores = nt(key_ref[...], q_ref[...]) * features ** (-0.5)
    scores = jnp.concatenate(
        [
            jnp.where(slot_hit(links, s), scores[s * BR : (s + 1) * BR], -jnp.inf)
            for s in range(slots)
        ],
        axis=0,
    )
    own_top = stat_ref[0:1]
    top = jnp.maximum(own_top, jnp.max(scores, axis=0, keepdims=True))
    powers = jnp.exp(scores - top)
    lower = jnp.exp(own_top - top)
    inverse = MIXING / (lower * stat_ref[1:2] + jnp.sum(powers, axis=0, keepdims=True))
    lower = lower * inverse
    powers = powers.astype(BF)
    p_ref[...] = powers
    out_ref[...] = jnp.concatenate([lower, inverse, jnp.zeros((6, QB), F32)], axis=0)
    near = nn(got_ref[:, :SUB, :].reshape(relays * SUB, slots * BR), powers)
    sharp = sharpened(mix_ref[...] * lower + near * inverse, prior_ref)
    lab_ref[...] = padded(sharp, relays * SUB).astype(BF)


def sharpened(mixed, prior_ref):
    share = share_of(prior_ref)
    mixed = mixed[: share.shape[0]] + (1.0 - MIXING) * share
    squared = mixed * mixed
    return squared / jnp.sum(squared, axis=0, keepdims=True)


def near_part(got, emb, links_t, mix, stat, prior_t):
    rows, features = emb.shape
    relays, depth2, near_keys = got.shape
    classes = prior_t.shape[0]
    depth = relays * SUB
    return pl.pallas_call(
        near_kernel,
        grid=(rows // QB,),
        in_specs=[
            pl.BlockSpec((relays, depth2, near_keys), lambda i: (0, 0, 0)),
            pl.BlockSpec((QB, features), lambda i: (i, 0)),
            pl.BlockSpec((links_t.shape[0], QB), lambda i: (0, i)),
            pl.BlockSpec((depth, QB), lambda i: (0, i)),
            pl.BlockSpec((8, QB), lambda i: (0, i)),
            pl.BlockSpec((classes, QB), lambda i: (0, i)),
        ],
        out_specs=[
            pl.BlockSpec((depth, QB), lambda i: (0, i)),
            pl.BlockSpec((near_keys, QB), lambda i: (0, i)),
            pl.BlockSpec((8, QB), lambda i: (0, i)),
        ],
        out_shape=[
            jax.ShapeDtypeStruct((depth, rows), BF),
            jax.ShapeDtypeStruct((near_keys, rows), BF),
            jax.ShapeDtypeStruct((8, rows), F32),
        ],
        scratch_shapes=[pltpu.VMEM((near_keys, features), BF)],
        compiler_params=params(),
        cost_estimate=cost(4 * near_keys * rows * features, 12 * depth * rows, near_keys * rows),
        name="near_part",
    )(got, emb, links_t, mix, stat, prior_t)


def remix_kernel(lab_ref, below_ref, above_ref, p_ref, out_ref):
    rows = lab_ref.shape[1]
    far = jnp.concatenate([below_ref[...], above_ref[...]], axis=1)
    out_ref[...] = nn(lab_ref[...], p_ref[:rows]) + nn(far, p_ref[rows:])


def remix(labels_t, below, above, powers):
    depth, rows = labels_t.shape
    keys = powers.shape[0]
    return pl.pallas_call(
        remix_kernel,
        grid=(rows // QB,),
        in_specs=[
            pl.BlockSpec((depth, rows), lambda i: (0, 0)),
            pl.BlockSpec((depth, BR), lambda i: (0, 0)),
            pl.BlockSpec((depth, BR), lambda i: (0, 0)),
            pl.BlockSpec((keys, QB), lambda i: (0, i)),
        ],
        out_specs=pl.BlockSpec((depth, QB), lambda i: (0, i)),
        out_shape=jax.ShapeDtypeStruct((depth, rows), F32),
        compiler_params=params(),
        cost_estimate=cost(2 * keys * rows * depth, 8 * depth * rows),
        name="remix",
    )(labels_t, below, above, powers)


def last_kernel(got_ref, p_ref, mix_ref, scale_ref, prior_ref, out_ref):
    relays, sub, near_keys = got_ref.shape
    near = nn(got_ref[...].reshape(relays * sub, near_keys), p_ref[...])
    mixed = mix_ref[...] * scale_ref[0:1] + near * scale_ref[1:2]
    sharp = sharpened(mixed, prior_ref)
    out_ref[...] = sharp * float(out_ref.shape[0])


def last_part(got, powers, mix, scales, prior_t):
    relays, sub, near_keys = got.shape
    classes, rows = prior_t.shape
    depth = relays * sub
    return pl.pallas_call(
        last_kernel,
        grid=(rows // QB,),
        in_specs=[
            pl.BlockSpec((relays, sub, near_keys), lambda i: (0, 0, 0)),
            pl.BlockSpec((near_keys, QB), lambda i: (0, i)),
            pl.BlockSpec((depth, QB), lambda i: (0, i)),
            pl.BlockSpec((8, QB), lambda i: (0, i)),
            pl.BlockSpec((classes, QB), lambda i: (0, i)),
        ],
        out_specs=pl.BlockSpec((classes, QB), lambda i: (0, i)),
        out_shape=jax.ShapeDtypeStruct((classes, rows), F32),
        compiler_params=params(),
        cost_estimate=cost(2 * near_keys * rows * depth, 12 * depth * rows),
        name="last_part",
    )(got, powers, mix, scales, prior_t)


def exchanged(x):
    return lax.all_to_all(x, "member", split_axis=0, concat_axis=0, tiled=True)


def body(embeddings, prior, source_member, source_block, cross_block, row_links):
    relays = lax.axis_size("member")
    groups = lax.axis_size("group")
    group = lax.axis_index("group")
    rows = embeddings.shape[0]
    owners, blocks = source_member[0], source_block[0]
    near_slots = owners.shape[1]
    prior_t, links_t = prior.T, row_links.T
    up = [(i, (i + 1) % groups) for i in range(groups)]
    down = [(j, i) for i, j in up]
    asked = cross_block[:, 0, :]
    to_above = lax.dynamic_slice(asked, ((group + 1) % groups, 0), (1, 1)).reshape(1)
    to_below = lax.dynamic_slice(asked, ((group + groups - 1) % groups, 1), (1, 1)).reshape(1)

    spread = prep(prior_t, embeddings, relays)
    relayed = exchanged(spread)
    below = lax.ppermute(pack(to_above, embeddings, spread), "group", up)
    above = lax.ppermute(pack(to_below, embeddings, spread), "group", down)
    far_powers, mix, stat = own_part(embeddings, spread, below, above, links_t, near_slots)
    near = exchanged(select(owners, blocks, relayed, stat))
    labels_t, near_powers, scales = near_part(near, embeddings, links_t, mix, stat, prior_t)

    relayed = exchanged(labels_t.reshape(relays, SUB, rows))
    below = lax.ppermute(pack_labels(to_above, labels_t), "group", up)
    above = lax.ppermute(pack_labels(to_below, labels_t), "group", down)
    mix = remix(labels_t, below, above, far_powers)
    near = exchanged(select(owners, blocks, relayed, mix))
    return last_part(near, near_powers, mix, scales, prior_t).T


def solution(mesh):
    placed = (
        P(("group", "member"), None),
        P(("group", "member"), None),
        P("group", None, None),
        P("group", None, None),
        P(None, "member", None),
        P(("group", "member"), None),
    )
    return jax.shard_map(
        body, mesh=mesh, in_specs=placed, out_specs=P(("group", "member"), None), check_vma=False
    )
```

```python
import jax
import jax.numpy as jnp
from jax import lax
from jax.experimental import pallas as pl
from jax.experimental.pallas import tpu as pltpu
from jax.sharding import PartitionSpec as P

BR = 128
MIXING = 0.8
SUB = 32
QB = 256
PARTS = 5
STORES = 4
BF = jnp.bfloat16
F32 = jnp.float32
VMEM_BYTES = 24 * 1024 * 1024


def params():
    return pltpu.CompilerParams(
        dimension_semantics=("arbitrary",), vmem_limit_bytes=VMEM_BYTES
    )


def in_hbm(x):
    return pltpu.with_memory_space_constraint(x, pltpu.HBM)


def in_vmem(x):
    return pltpu.with_memory_space_constraint(x, pltpu.VMEM)


def cost(flops, size, exps=0):
    return pl.CostEstimate(flops=flops, bytes_accessed=size, transcendentals=exps)


def nt(a, b):
    return lax.dot_general(a, b, (((1,), (1,)), ((), ())), preferred_element_type=F32)


def nn(a, b):
    return jnp.dot(a, b, preferred_element_type=F32)


def padded(x, rows):
    if x.shape[0] == rows:
        return x
    return jnp.concatenate([x, jnp.zeros((rows - x.shape[0], x.shape[1]), x.dtype)], axis=0)


def prep_kernel(prior_ref, emb_ref, out_ref, prior_buf, emb_buf, out_buf, sem_p, sem_e, sem_o):
    relays, _, rows = out_ref.shape
    classes, features = prior_ref.shape[0], emb_ref.shape[1]
    wide, tall = features // BR, BR // SUB
    part = classes // PARTS
    loads = [
        pltpu.make_async_copy(
            prior_ref.at[pl.ds(i * part, part)], prior_buf.at[pl.ds(i * part, part)], sem_p.at[i]
        )
        for i in range(PARTS)
    ]
    pieces = [
        pltpu.make_async_copy(emb_ref.at[pl.ds(b * BR, BR)], emb_buf.at[pl.ds(b * BR, BR)], sem_e.at[b])
        for b in range(rows // BR)
    ]
    for copy in (*pieces, *loads):
        copy.start()
    for b, copy in enumerate(pieces):
        copy.wait()
        for r in range(tall):
            at = b * BR + r * SUB
            for f in range(wide):
                out_buf[r * wide + f, SUB:, b * BR : (b + 1) * BR] = emb_buf[
                    at : at + SUB, f * BR : (f + 1) * BR
                ]
    total = jnp.zeros((8, rows), F32)
    for i, copy in enumerate(loads):
        copy.wait()
        rest = prior_buf[i * part : (i + 1) * part].reshape(part // 8, 8, rows)
        total = total + jnp.sum(rest, axis=0)
    inverse = 1.0 / jnp.sum(total, axis=0, keepdims=True)
    batch = relays // STORES
    stores = []
    for i in range(STORES):
        for m in range(i * batch, (i + 1) * batch):
            end = min(classes, (m + 1) * SUB)
            share = padded(prior_buf[m * SUB : end] * inverse, SUB)
            out_buf[m, :SUB, :] = share.astype(BF)
        stores.append(
            pltpu.make_async_copy(
                out_buf.at[pl.ds(i * batch, batch)], out_ref.at[pl.ds(i * batch, batch)], sem_o.at[i]
            )
        )
        stores[-1].start()
    for copy in stores:
        copy.wait()


def prep(prior_t, emb, relays):
    classes, rows = prior_t.shape
    features = emb.shape[1]
    shape = (relays, 2 * SUB, rows)
    return pl.pallas_call(
        prep_kernel,
        in_specs=[pl.BlockSpec(memory_space=pl.ANY)] * 2,
        out_specs=pl.BlockSpec(memory_space=pl.ANY),
        out_shape=jax.ShapeDtypeStruct(shape, BF),
        scratch_shapes=[
            pltpu.VMEM((classes, rows), F32),
            pltpu.VMEM((rows, features), BF),
            pltpu.VMEM(shape, BF),
            pltpu.SemaphoreType.DMA((PARTS,)),
            pltpu.SemaphoreType.DMA((rows // BR,)),
            pltpu.SemaphoreType.DMA((STORES,)),
        ],
        compiler_params=pltpu.CompilerParams(vmem_limit_bytes=VMEM_BYTES),
        cost_estimate=cost(4 * classes * rows, 4 * classes * rows + 4 * features * rows),
        name="prep",
    )(in_hbm(prior_t), in_hbm(emb))


def select_kernel(owner_ref, block_ref, got_ref, after_ref, out_ref):
    members, slots = owner_ref.shape

    @pl.loop(0, members, unroll=8)
    def _(d):
        for k in range(slots):
            lane = pl.multiple_of(block_ref[d, k] * BR, BR)
            out_ref[d, :, k * BR : (k + 1) * BR] = got_ref[owner_ref[d, k], :, pl.ds(lane, BR)]


def select(owners, blocks, got, after):
    members, slots = owners.shape
    depth = got.shape[1]
    return pl.pallas_call(
        select_kernel,
        in_specs=[
            pl.BlockSpec(memory_space=pltpu.SMEM),
            pl.BlockSpec(memory_space=pltpu.SMEM),
            pl.BlockSpec(memory_space=pltpu.VMEM),
            pl.BlockSpec(memory_space=pl.ANY),
        ],
        out_specs=pl.BlockSpec(memory_space=pltpu.VMEM),
        out_shape=jax.ShapeDtypeStruct((members, depth, slots * BR), BF),
        compiler_params=pltpu.CompilerParams(vmem_limit_bytes=VMEM_BYTES),
        cost_estimate=cost(0, 4 * got.size),
        name="select",
    )(owners, blocks, in_vmem(got), after)


def pack_kernel(pick_ref, emb_ref, lab_ref, out_ref):
    out_ref[:BR] = emb_ref[...]
    labels = lab_ref[...].reshape(-1, BR)
    for f in range(labels.shape[0] // BR):
        out_ref[BR:, f * BR : (f + 1) * BR] = labels[f * BR : (f + 1) * BR]


def pack(pick, emb, spread):
    relays = spread.shape[0]
    features = emb.shape[1]
    return pl.pallas_call(
        pack_kernel,
        grid_spec=pltpu.PrefetchScalarGridSpec(
            num_scalar_prefetch=1,
            grid=(1,),
            in_specs=[
                pl.BlockSpec((BR, features), lambda i, p: (p[0], 0)),
                pl.BlockSpec((relays, SUB, BR), lambda i, p: (0, 0, p[0])),
            ],
            out_specs=pl.BlockSpec((2 * BR, features), lambda i, p: (0, 0)),
        ),
        out_shape=jax.ShapeDtypeStruct((2 * BR, features), BF),
        compiler_params=params(),
        cost_estimate=cost(0, 8 * BR * features),
        name="pack_cross",
    )(pick, emb, spread)


def pack_labels_kernel(pick_ref, lab_ref, out_ref):
    out_ref[...] = lab_ref[...]


def pack_labels(pick, labels_t):
    depth = labels_t.shape[0]
    return pl.pallas_call(
        pack_labels_kernel,
        grid_spec=pltpu.PrefetchScalarGridSpec(
            num_scalar_prefetch=1,
            grid=(1,),
            in_specs=[pl.BlockSpec((depth, BR), lambda i, p: (0, p[0]))],
            out_specs=pl.BlockSpec((depth, BR), lambda i, p: (0, 0)),
        ),
        out_shape=jax.ShapeDtypeStruct((depth, BR), BF),
        compiler_params=params(),
        cost_estimate=cost(0, 4 * BR * depth),
        name="pack_labels",
    )(pick, labels_t)


def slot_hit(links, slot):
    return jnp.max(jnp.where(links == slot, 1.0, 0.0), axis=0, keepdims=True) > 0.0


def own_kernel(near_slots, emb_ref, q_ref, lab_ref, below_ref, above_ref, links_ref, p_ref, mix_ref, stat_ref, far_ref):
    step = pl.program_id(0)
    rows, features = emb_ref.shape
    depth = mix_ref.shape[0]

    @pl.when(step == 0)
    def _():
        for f in range(depth // BR):
            for s, ref in enumerate((below_ref, above_ref)):
                far_ref[f * BR : (f + 1) * BR, s * BR : (s + 1) * BR] = ref[BR:, f * BR : (f + 1) * BR]

    q = q_ref[...]
    scale = features ** (-0.5)
    own = nt(emb_ref[...], q) * scale
    key_id = lax.broadcasted_iota(jnp.int32, own.shape, 0)
    row_id = lax.broadcasted_iota(jnp.int32, own.shape, 1) + step * QB
    own = jnp.where(key_id == row_id, -jnp.inf, own)
    links = links_ref[...]
    parts = [own]
    for s, ref in enumerate((below_ref, above_ref)):
        far = nt(ref[:BR], q) * scale
        parts.append(jnp.where(slot_hit(links, near_slots + s), far, -jnp.inf))
    scores = jnp.concatenate(parts, axis=0)
    top = jnp.max(scores, axis=0, keepdims=True)
    powers = jnp.exp(scores - top)
    total = jnp.sum(powers, axis=0, keepdims=True)
    powers = powers.astype(BF)
    p_ref[...] = powers
    mix_ref[...] = nn(lab_ref[...].reshape(depth, rows), powers[:rows]) + nn(far_ref[...], powers[rows:])
    stat_ref[...] = jnp.concatenate([top, total, jnp.zeros((6, QB), F32)], axis=0)


def own_part(emb, spread, below, above, links_t, near_slots):
    rows, features = emb.shape
    relays = spread.shape[0]
    depth = relays * SUB
    keys = rows + 2 * BR
    return pl.pallas_call(
        lambda *refs: own_kernel(near_slots, *refs),
        grid=(rows // QB,),
        in_specs=[
            pl.BlockSpec((rows, features), lambda i: (0, 0)),
            pl.BlockSpec((QB, features), lambda i: (i, 0)),
            pl.BlockSpec((relays, SUB, rows), lambda i: (0, 0, 0)),
            pl.BlockSpec((2 * BR, features), lambda i: (0, 0)),
            pl.BlockSpec((2 * BR, features), lambda i: (0, 0)),
            pl.BlockSpec((links_t.shape[0], QB), lambda i: (0, i)),
        ],
        out_specs=[
            pl.BlockSpec((keys, QB), lambda i: (0, i)),
            pl.BlockSpec((depth, QB), lambda i: (0, i)),
            pl.BlockSpec((8, QB), lambda i: (0, i)),
        ],
        out_shape=[
            pltpu.HBM((keys, rows), BF),
            pltpu.HBM((depth, rows), F32),
            jax.ShapeDtypeStruct((8, rows), F32),
        ],
        scratch_shapes=[pltpu.VMEM((depth, 2 * BR), BF)],
        compiler_params=params(),
        cost_estimate=cost(4 * keys * rows * features, 12 * depth * rows, keys * rows),
        name="own_part",
    )(emb, emb, spread, below, above, links_t)


def near_kernel(
    got_ref, emb_ref, links_ref, mix_ref, stat_ref, prior_ref,
    lab_ref, p_ref, out_ref,
    key_ref, lab_buf, p_buf, sem_l, sem_p,
):
    rows, features = emb_ref.shape
    relays = got_ref.shape[0]
    slots = got_ref.shape[2] // BR
    wide = features // BR
    for s in range(slots):
        for r in range(BR // SUB):
            at = s * BR + r * SUB
            for f in range(wide):
                key_ref[at : at + SUB, f * BR : (f + 1) * BR] = got_ref[
                    r * wide + f, SUB:, s * BR : (s + 1) * BR
                ]
    near_labels = got_ref[:, :SUB, :].reshape(relays * SUB, slots * BR)
    copies = []
    for i in range(rows // QB):
        at = slice(i * QB, (i + 1) * QB)
        links = links_ref[:, at]
        scores = nt(key_ref[...], emb_ref[at]) * features ** (-0.5)
        scores = jnp.concatenate(
            [
                jnp.where(slot_hit(links, s), scores[s * BR : (s + 1) * BR], -jnp.inf)
                for s in range(slots)
            ],
            axis=0,
        )
        own_top = stat_ref[0:1, at]
        top = jnp.maximum(own_top, jnp.max(scores, axis=0, keepdims=True))
        powers = jnp.exp(scores - top)
        lower = jnp.exp(own_top - top)
        total = lower * stat_ref[1:2, at] + jnp.sum(powers, axis=0, keepdims=True)
        inverse = MIXING / total
        lower = lower * inverse
        powers = powers.astype(BF)
        p_buf[i] = powers
        out_ref[:, at] = jnp.concatenate([lower, inverse, jnp.zeros((6, QB), F32)], axis=0)
        near = nn(near_labels, powers)
        sharp = sharpened(mix_ref[:, at] * lower + near * inverse, prior_ref[:, at])
        lab_buf[i] = padded(sharp, relays * SUB).astype(BF)
        copies.append(pltpu.make_async_copy(lab_buf.at[i], lab_ref.at[:, pl.ds(i * QB, QB)], sem_l.at[i]))
        copies.append(pltpu.make_async_copy(p_buf.at[i], p_ref.at[:, pl.ds(i * QB, QB)], sem_p.at[i]))
        copies[-2].start()
        copies[-1].start()
    for copy in copies:
        copy.wait()


def sharpened(mixed, prior):
    share = prior * (1.0 / jnp.sum(prior, axis=0, keepdims=True))
    mixed = mixed[: share.shape[0]] + (1.0 - MIXING) * share
    squared = mixed * mixed
    return squared * (1.0 / jnp.sum(squared, axis=0, keepdims=True))


def near_part(got, emb, links_t, mix, stat, prior_t):
    rows, features = emb.shape
    relays, _, near_keys = got.shape
    depth, steps = relays * SUB, rows // QB
    whole = pl.BlockSpec(memory_space=pltpu.VMEM)
    return pl.pallas_call(
        near_kernel,
        in_specs=[whole] * 6,
        out_specs=[pl.BlockSpec(memory_space=pl.ANY)] * 2 + [whole],
        out_shape=[
            pltpu.HBM((depth, rows), BF),
            pltpu.HBM((near_keys, rows), BF),
            jax.ShapeDtypeStruct((8, rows), F32),
        ],
        scratch_shapes=[
            pltpu.VMEM((near_keys, features), BF),
            pltpu.VMEM((steps, depth, QB), BF),
            pltpu.VMEM((steps, near_keys, QB), BF),
            pltpu.SemaphoreType.DMA((steps,)),
            pltpu.SemaphoreType.DMA((steps,)),
        ],
        compiler_params=pltpu.CompilerParams(vmem_limit_bytes=VMEM_BYTES),
        cost_estimate=cost(4 * near_keys * rows * features, 12 * depth * rows, near_keys * rows),
        name="near_part",
    )(got, emb, links_t, mix, stat, prior_t)


def remix_kernel(lab_ref, below_ref, above_ref, p_ref, out_ref):
    rows = lab_ref.shape[1]
    far = jnp.concatenate([below_ref[...], above_ref[...]], axis=1)
    out_ref[...] = nn(lab_ref[...], p_ref[:rows]) + nn(far, p_ref[rows:])


def remix(labels_t, below, above, powers):
    depth, rows = labels_t.shape
    keys = powers.shape[0]
    return pl.pallas_call(
        remix_kernel,
        grid=(rows // QB,),
        in_specs=[
            pl.BlockSpec((depth, rows), lambda i: (0, 0)),
            pl.BlockSpec((depth, BR), lambda i: (0, 0)),
            pl.BlockSpec((depth, BR), lambda i: (0, 0)),
            pl.BlockSpec((keys, QB), lambda i: (0, i)),
        ],
        out_specs=pl.BlockSpec((depth, QB), lambda i: (0, i)),
        out_shape=jax.ShapeDtypeStruct((depth, rows), F32),
        compiler_params=params(),
        cost_estimate=cost(2 * keys * rows * depth, 8 * depth * rows),
        name="remix",
    )(labels_t, below, above, powers)


def last_kernel(got_ref, p_ref, mix_ref, scale_ref, prior_ref, out_ref, buf, sem):
    relays, sub, near_keys = got_ref.shape
    classes, rows = prior_ref.shape
    near_labels = got_ref[...].reshape(relays * sub, near_keys)
    copies = []
    for i in range(rows // QB):
        at = slice(i * QB, (i + 1) * QB)
        near = nn(near_labels, p_ref[:, at])
        mixed = mix_ref[:, at] * scale_ref[0:1, at] + near * scale_ref[1:2, at]
        buf[i] = sharpened(mixed, prior_ref[:, at]) * float(classes)
        copies.append(pltpu.make_async_copy(buf.at[i], out_ref.at[:, pl.ds(i * QB, QB)], sem.at[i]))
        copies[-1].start()
    for copy in copies:
        copy.wait()


def last_part(got, powers, mix, scales, prior_t):
    relays, sub, near_keys = got.shape
    classes, rows = prior_t.shape
    depth, steps = relays * sub, rows // QB
    return pl.pallas_call(
        last_kernel,
        in_specs=[pl.BlockSpec(memory_space=pltpu.VMEM)] * 5,
        out_specs=pl.BlockSpec(memory_space=pl.ANY),
        out_shape=jax.ShapeDtypeStruct((classes, rows), F32),
        scratch_shapes=[
            pltpu.VMEM((steps, classes, QB), F32),
            pltpu.SemaphoreType.DMA((steps,)),
        ],
        compiler_params=pltpu.CompilerParams(vmem_limit_bytes=VMEM_BYTES),
        cost_estimate=cost(2 * near_keys * rows * depth, 12 * depth * rows),
        name="last_part",
    )(got, powers, mix, scales, prior_t)


def exchanged(x):
    return lax.all_to_all(x, "member", split_axis=0, concat_axis=0, tiled=True)


def body(embeddings, prior, source_member, source_block, cross_block, row_links):
    relays = lax.axis_size("member")
    groups = lax.axis_size("group")
    group = lax.axis_index("group")
    rows = embeddings.shape[0]
    owners, blocks = source_member[0], source_block[0]
    near_slots = owners.shape[1]
    prior_t, links_t = prior.T, row_links.T
    up = [(i, (i + 1) % groups) for i in range(groups)]
    down = [(j, i) for i, j in up]
    asked = cross_block[:, 0, :]
    to_above = lax.dynamic_slice(asked, ((group + 1) % groups, 0), (1, 1)).reshape(1)
    to_below = lax.dynamic_slice(asked, ((group + groups - 1) % groups, 1), (1, 1)).reshape(1)

    spread = prep(prior_t, embeddings, relays)
    relayed = exchanged(spread)
    below = lax.ppermute(pack(to_above, embeddings, spread), "group", up)
    above = lax.ppermute(pack(to_below, embeddings, spread), "group", down)
    far_powers, mix, stat = own_part(embeddings, spread, below, above, links_t, near_slots)
    near = exchanged(select(owners, blocks, relayed, stat))
    labels_t, near_powers, scales = near_part(near, embeddings, links_t, mix, stat, prior_t)

    relayed = exchanged(labels_t.reshape(relays, SUB, rows))
    below = lax.ppermute(pack_labels(to_above, labels_t), "group", up)
    above = lax.ppermute(pack_labels(to_below, labels_t), "group", down)
    mix = remix(labels_t, below, above, far_powers)
    near = exchanged(select(owners, blocks, relayed, mix))
    return last_part(near, near_powers, mix, scales, prior_t).T


def solution(mesh):
    placed = (
        P(("group", "member"), None),
        P(("group", "member"), None),
        P("group", None, None),
        P("group", None, None),
        P(None, "member", None),
        P(("group", "member"), None),
    )
    return jax.shard_map(
        body, mesh=mesh, in_specs=placed, out_specs=P(("group", "member"), None), check_vma=False
    )
```

```python
import jax
import jax.numpy as jnp
from jax import lax
from jax.experimental import pallas as pl
from jax.experimental.pallas import tpu as pltpu
from jax.sharding import PartitionSpec as P

BR = 128
MIXING = 0.8
SUB = 32
QB = 256
PARTS = 5
STORES = 4
BF = jnp.bfloat16
F32 = jnp.float32
VMEM_BYTES = 24 * 1024 * 1024


def params():
    return pltpu.CompilerParams(
        dimension_semantics=("arbitrary",), vmem_limit_bytes=VMEM_BYTES
    )


def in_hbm(x):
    return pltpu.with_memory_space_constraint(x, pltpu.HBM)


def cost(flops, size, exps=0):
    return pl.CostEstimate(flops=flops, bytes_accessed=size, transcendentals=exps)


def nn(a, b):
    return jnp.dot(a, b, preferred_element_type=F32)


def padded(x, rows):
    if x.shape[0] == rows:
        return x
    return jnp.concatenate([x, jnp.zeros((rows - x.shape[0], x.shape[1]), x.dtype)], axis=0)


def prep_kernel(prior_ref, emb_ref, out_ref, prior_buf, emb_buf, out_buf, sem_p, sem_e, sem_o):
    relays, _, rows = out_ref.shape
    classes, features = prior_ref.shape[0], emb_ref.shape[1]
    wide, tall = features // BR, BR // SUB
    part = classes // PARTS
    loads = [
        pltpu.make_async_copy(
            prior_ref.at[pl.ds(i * part, part)], prior_buf.at[pl.ds(i * part, part)], sem_p.at[i]
        )
        for i in range(PARTS)
    ]
    pieces = [
        pltpu.make_async_copy(emb_ref.at[pl.ds(b * BR, BR)], emb_buf.at[pl.ds(b * BR, BR)], sem_e.at[b])
        for b in range(rows // BR)
    ]
    for copy in (*pieces, *loads):
        copy.start()
    for b, copy in enumerate(pieces):
        copy.wait()
        for r in range(tall):
            at = b * BR + r * SUB
            for f in range(wide):
                out_buf[r * wide + f, SUB:, b * BR : (b + 1) * BR] = emb_buf[
                    at : at + SUB, f * BR : (f + 1) * BR
                ]
    stores = [
        pltpu.make_async_copy(
            out_buf.at[:, pl.ds(SUB, SUB)], out_ref.at[:, pl.ds(SUB, SUB)], sem_o.at[STORES]
        )
    ]
    stores[0].start()
    total = jnp.zeros((8, rows), F32)
    for i, copy in enumerate(loads):
        copy.wait()
        rest = prior_buf[i * part : (i + 1) * part].reshape(part // 8, 8, rows)
        total = total + jnp.sum(rest, axis=0)
    inverse = 1.0 / jnp.sum(total, axis=0, keepdims=True)
    batch = relays // STORES
    for i in range(STORES):
        for m in range(i * batch, (i + 1) * batch):
            end = min(classes, (m + 1) * SUB)
            share = padded(prior_buf[m * SUB : end] * inverse, SUB)
            out_buf[m, :SUB, :] = share.astype(BF)
        stores.append(
            pltpu.make_async_copy(
                out_buf.at[pl.ds(i * batch, batch), pl.ds(0, SUB)],
                out_ref.at[pl.ds(i * batch, batch), pl.ds(0, SUB)],
                sem_o.at[i],
            )
        )
        stores[-1].start()
    for copy in stores:
        copy.wait()


def prep(prior_t, emb, relays):
    classes, rows = prior_t.shape
    features = emb.shape[1]
    shape = (relays, 2 * SUB, rows)
    return pl.pallas_call(
        prep_kernel,
        in_specs=[pl.BlockSpec(memory_space=pl.ANY)] * 2,
        out_specs=pl.BlockSpec(memory_space=pl.ANY),
        out_shape=jax.ShapeDtypeStruct(shape, BF),
        scratch_shapes=[
            pltpu.VMEM((classes, rows), F32),
            pltpu.VMEM((rows, features), BF),
            pltpu.VMEM(shape, BF),
            pltpu.SemaphoreType.DMA((PARTS,)),
            pltpu.SemaphoreType.DMA((rows // BR,)),
            pltpu.SemaphoreType.DMA((STORES + 1,)),
        ],
        compiler_params=pltpu.CompilerParams(vmem_limit_bytes=VMEM_BYTES),
        cost_estimate=cost(4 * classes * rows, 4 * classes * rows + 4 * features * rows),
        name="prep",
    )(in_hbm(prior_t), in_hbm(emb))


def select_kernel(owner_ref, block_ref, got_ref, after_ref, out_ref):
    members, slots = owner_ref.shape

    @pl.loop(0, members, unroll=8)
    def _(d):
        for k in range(slots):
            lane = pl.multiple_of(block_ref[d, k] * BR, BR)
            out_ref[d, :, k * BR : (k + 1) * BR] = got_ref[owner_ref[d, k], :, pl.ds(lane, BR)]


def select(owners, blocks, got, after):
    members, slots = owners.shape
    depth = got.shape[1]
    return pl.pallas_call(
        select_kernel,
        in_specs=[
            pl.BlockSpec(memory_space=pltpu.SMEM),
            pl.BlockSpec(memory_space=pltpu.SMEM),
            pl.BlockSpec(memory_space=pltpu.VMEM),
            pl.BlockSpec(memory_space=pl.ANY),
        ],
        out_specs=pl.BlockSpec(memory_space=pltpu.VMEM),
        out_shape=jax.ShapeDtypeStruct((members, depth, slots * BR), BF),
        compiler_params=pltpu.CompilerParams(vmem_limit_bytes=VMEM_BYTES),
        cost_estimate=cost(0, 4 * got.size),
        name="select",
    )(owners, blocks, got, after)


def pack_kernel(pick_ref, emb_ref, lab_ref, out_ref):
    out_ref[:BR] = emb_ref[...]
    labels = lab_ref[...].reshape(-1, BR)
    for f in range(labels.shape[0] // BR):
        out_ref[BR:, f * BR : (f + 1) * BR] = labels[f * BR : (f + 1) * BR]


def pack(pick, emb, spread):
    relays = spread.shape[0]
    features = emb.shape[1]
    return pl.pallas_call(
        pack_kernel,
        grid_spec=pltpu.PrefetchScalarGridSpec(
            num_scalar_prefetch=1,
            grid=(1,),
            in_specs=[
                pl.BlockSpec((BR, features), lambda i, p: (p[0], 0)),
                pl.BlockSpec((relays, SUB, BR), lambda i, p: (0, 0, p[0])),
            ],
            out_specs=pl.BlockSpec((2 * BR, features), lambda i, p: (0, 0)),
        ),
        out_shape=jax.ShapeDtypeStruct((2 * BR, features), BF),
        compiler_params=params(),
        cost_estimate=cost(0, 8 * BR * features),
        name="pack_cross",
    )(pick, in_hbm(emb), spread)


def pack_labels_kernel(pick_ref, lab_ref, out_ref):
    out_ref[...] = lab_ref[...]


def pack_labels(pick, labels_t):
    depth = labels_t.shape[0]
    return pl.pallas_call(
        pack_labels_kernel,
        grid_spec=pltpu.PrefetchScalarGridSpec(
            num_scalar_prefetch=1,
            grid=(1,),
            in_specs=[pl.BlockSpec((depth, BR), lambda i, p: (0, p[0]))],
            out_specs=pl.BlockSpec((depth, BR), lambda i, p: (0, 0)),
        ),
        out_shape=jax.ShapeDtypeStruct((depth, BR), BF),
        compiler_params=params(),
        cost_estimate=cost(0, 4 * BR * depth),
        name="pack_labels",
    )(pick, labels_t)


def slot_hit(links, slot):
    return jnp.max(jnp.where(links == slot, 1.0, 0.0), axis=0, keepdims=True) > 0.0


def own_kernel(near_slots, emb_ref, q_ref, lab_ref, below_ref, above_ref, links_ref, prior_ref, p_ref, mix_ref, stat_ref, turned_ref, far_ref):
    step = pl.program_id(0)
    rows, features = emb_ref.shape
    depth = mix_ref.shape[0]

    @pl.when(step == 0)
    def _():
        for f in range(depth // BR):
            for s, ref in enumerate((below_ref, above_ref)):
                far_ref[f * BR : (f + 1) * BR, s * BR : (s + 1) * BR] = ref[BR:, f * BR : (f + 1) * BR]

    q = q_ref[...].T
    turned_ref[...] = q
    scale = features ** (-0.5)
    own = nn(emb_ref[...], q) * scale
    key_id = lax.broadcasted_iota(jnp.int32, own.shape, 0)
    row_id = lax.broadcasted_iota(jnp.int32, own.shape, 1) + step * QB
    own = jnp.where(key_id == row_id, -jnp.inf, own)
    links = links_ref[...]
    parts = [own]
    for s, ref in enumerate((below_ref, above_ref)):
        far = nn(ref[:BR], q) * scale
        parts.append(jnp.where(slot_hit(links, near_slots + s), far, -jnp.inf))
    scores = jnp.concatenate(parts, axis=0)
    top = jnp.max(scores, axis=0, keepdims=True)
    powers = jnp.exp(scores - top)
    total = jnp.sum(powers, axis=0, keepdims=True)
    powers = powers.astype(BF)
    p_ref[...] = powers
    mix_ref[...] = nn(lab_ref[...].reshape(depth, rows), powers[:rows]) + nn(far_ref[...], powers[rows:])
    share = (1.0 - MIXING) / jnp.sum(prior_ref[...], axis=0, keepdims=True)
    stat_ref[...] = jnp.concatenate([top, total, share, jnp.zeros((5, QB), F32)], axis=0)


def own_part(emb, spread, below, above, links_t, prior_t, near_slots):
    rows, features = emb.shape
    relays = spread.shape[0]
    depth = relays * SUB
    keys = rows + 2 * BR
    return pl.pallas_call(
        lambda *refs: own_kernel(near_slots, *refs),
        grid=(rows // QB,),
        in_specs=[
            pl.BlockSpec((rows, features), lambda i: (0, 0)),
            pl.BlockSpec((QB, features), lambda i: (i, 0)),
            pl.BlockSpec((relays, SUB, rows), lambda i: (0, 0, 0)),
            pl.BlockSpec((2 * BR, features), lambda i: (0, 0)),
            pl.BlockSpec((2 * BR, features), lambda i: (0, 0)),
            pl.BlockSpec((links_t.shape[0], QB), lambda i: (0, i)),
            pl.BlockSpec((prior_t.shape[0], QB), lambda i: (0, i)),
        ],
        out_specs=[
            pl.BlockSpec((keys, QB), lambda i: (0, i)),
            pl.BlockSpec((depth, QB), lambda i: (0, i)),
            pl.BlockSpec((8, QB), lambda i: (0, i)),
            pl.BlockSpec((features, QB), lambda i: (0, i)),
        ],
        out_shape=[
            pltpu.HBM((keys, rows), BF),
            pltpu.HBM((depth, rows), F32),
            jax.ShapeDtypeStruct((8, rows), F32),
            pltpu.HBM((features, rows), BF),
        ],
        scratch_shapes=[pltpu.VMEM((depth, 2 * BR), BF)],
        compiler_params=params(),
        cost_estimate=cost(4 * keys * rows * features, 12 * depth * rows, keys * rows),
        name="own_part",
    )(in_hbm(emb), in_hbm(emb), spread, below, above, links_t, in_hbm(prior_t))


def near_kernel(
    got_ref, turned_ref, links_ref, mix_ref, stat_ref, prior_ref,
    lab_ref, p_ref, out_ref,
    key_ref, mixed_buf, lab_buf, p_buf, sem_l, sem_p,
):
    features, rows = turned_ref.shape
    relays = got_ref.shape[0]
    slots = got_ref.shape[2] // BR
    wide = features // BR
    for s in range(slots):
        for r in range(BR // SUB):
            at = s * BR + r * SUB
            for f in range(wide):
                key_ref[at : at + SUB, f * BR : (f + 1) * BR] = got_ref[
                    r * wide + f, SUB:, s * BR : (s + 1) * BR
                ]
    near_labels = got_ref[:, :SUB, :].reshape(relays * SUB, slots * BR)
    copies = []
    for i in range(rows // QB):
        at = slice(i * QB, (i + 1) * QB)
        links = links_ref[:, at]
        scores = nn(key_ref[...], turned_ref[:, at]) * features ** (-0.5)
        scores = jnp.concatenate(
            [
                jnp.where(slot_hit(links, s), scores[s * BR : (s + 1) * BR], -jnp.inf)
                for s in range(slots)
            ],
            axis=0,
        )
        own_top = stat_ref[0:1, at]
        top = jnp.maximum(own_top, jnp.max(scores, axis=0, keepdims=True))
        powers = jnp.exp(scores - top)
        lower = jnp.exp(own_top - top)
        total = lower * stat_ref[1:2, at] + jnp.sum(powers, axis=0, keepdims=True)
        inverse = MIXING / total
        lower = lower * inverse
        powers = powers.astype(BF)
        p_buf[i] = powers
        share = stat_ref[2:3, at]
        out_ref[:, at] = jnp.concatenate([lower, inverse, share, jnp.zeros((5, QB), F32)], axis=0)
        mixed_buf[i] = nn(near_labels, powers)
        norm = squares(mixed_buf.at[i], mix_ref, prior_ref, at, lower, inverse, share)
        for start, end in tiles(prior_ref.shape[0]):
            sharp = padded(mixed_buf[i, start:end] * norm, BR)
            lab_buf[i, start : start + BR] = sharp.astype(BF)
        copies.append(pltpu.make_async_copy(lab_buf.at[i], lab_ref.at[:, pl.ds(i * QB, QB)], sem_l.at[i]))
        copies.append(pltpu.make_async_copy(p_buf.at[i], p_ref.at[:, pl.ds(i * QB, QB)], sem_p.at[i]))
        copies[-2].start()
        copies[-1].start()
    for copy in copies:
        copy.wait()


def tiles(classes):
    return [(start, min(start + BR, classes)) for start in range(0, classes, BR)]


def squares(buf, mix_ref, prior_ref, at, lower, inverse, share):
    total = jnp.zeros((8, QB), F32)
    for start, end in tiles(prior_ref.shape[0]):
        mixed = mix_ref[start:end, at] * lower + buf[start:end] * inverse + prior_ref[start:end, at] * share
        mixed = mixed * mixed
        buf[start:end] = mixed
        total = total + jnp.sum(mixed.reshape(-1, 8, QB), axis=0)
    return 1.0 / jnp.sum(total, axis=0, keepdims=True)


def near_part(got, turned, links_t, mix, stat, prior_t):
    features, rows = turned.shape
    relays, _, near_keys = got.shape
    depth, steps = relays * SUB, rows // QB
    whole = pl.BlockSpec(memory_space=pltpu.VMEM)
    return pl.pallas_call(
        near_kernel,
        in_specs=[whole] * 6,
        out_specs=[pl.BlockSpec(memory_space=pl.ANY)] * 2 + [whole],
        out_shape=[
            pltpu.HBM((depth, rows), BF),
            pltpu.HBM((near_keys, rows), BF),
            jax.ShapeDtypeStruct((8, rows), F32),
        ],
        scratch_shapes=[
            pltpu.VMEM((near_keys, features), BF),
            pltpu.VMEM((steps, depth, QB), F32),
            pltpu.VMEM((steps, depth, QB), BF),
            pltpu.VMEM((steps, near_keys, QB), BF),
            pltpu.SemaphoreType.DMA((steps,)),
            pltpu.SemaphoreType.DMA((steps,)),
        ],
        compiler_params=pltpu.CompilerParams(vmem_limit_bytes=VMEM_BYTES),
        cost_estimate=cost(4 * near_keys * rows * features, 12 * depth * rows, near_keys * rows),
        name="near_part",
    )(got, turned, links_t, mix, stat, prior_t)


def remix_kernel(lab_ref, below_ref, above_ref, p_ref, out_ref):
    rows = lab_ref.shape[1]
    far = jnp.concatenate([below_ref[...], above_ref[...]], axis=1)
    out_ref[...] = nn(lab_ref[...], p_ref[:rows]) + nn(far, p_ref[rows:])


def remix(labels_t, below, above, powers):
    depth, rows = labels_t.shape
    keys = powers.shape[0]
    return pl.pallas_call(
        remix_kernel,
        grid=(rows // QB,),
        in_specs=[
            pl.BlockSpec((depth, rows), lambda i: (0, 0)),
            pl.BlockSpec((depth, BR), lambda i: (0, 0)),
            pl.BlockSpec((depth, BR), lambda i: (0, 0)),
            pl.BlockSpec((keys, QB), lambda i: (0, i)),
        ],
        out_specs=pl.BlockSpec((depth, QB), lambda i: (0, i)),
        out_shape=jax.ShapeDtypeStruct((depth, rows), F32),
        compiler_params=params(),
        cost_estimate=cost(2 * keys * rows * depth, 8 * depth * rows),
        name="remix",
    )(labels_t, below, above, powers)


def last_kernel(got_ref, p_ref, mix_ref, scale_ref, prior_ref, out_ref, mixed_buf, buf, sem):
    relays, sub, near_keys = got_ref.shape
    classes, rows = prior_ref.shape
    near_labels = got_ref[...].reshape(relays * sub, near_keys)
    copies = []
    for i in range(rows // QB):
        at = slice(i * QB, (i + 1) * QB)
        mixed_buf[i] = nn(near_labels, p_ref[:, at])
        scales = [scale_ref[k : k + 1, at] for k in range(3)]
        norm = squares(mixed_buf.at[i], mix_ref, prior_ref, at, *scales) * float(classes)
        for start, end in tiles(classes):
            buf[i, start:end] = mixed_buf[i, start:end] * norm
        copies.append(pltpu.make_async_copy(buf.at[i], out_ref.at[:, pl.ds(i * QB, QB)], sem.at[i]))
        copies[-1].start()
    for copy in copies:
        copy.wait()


def last_part(got, powers, mix, scales, prior_t):
    relays, sub, near_keys = got.shape
    classes, rows = prior_t.shape
    depth, steps = relays * sub, rows // QB
    return pl.pallas_call(
        last_kernel,
        in_specs=[pl.BlockSpec(memory_space=pltpu.VMEM)] * 5,
        out_specs=pl.BlockSpec(memory_space=pl.ANY),
        out_shape=jax.ShapeDtypeStruct((classes, rows), F32),
        scratch_shapes=[
            pltpu.VMEM((steps, depth, QB), F32),
            pltpu.VMEM((steps, classes, QB), F32),
            pltpu.SemaphoreType.DMA((steps,)),
        ],
        compiler_params=pltpu.CompilerParams(vmem_limit_bytes=VMEM_BYTES),
        cost_estimate=cost(2 * near_keys * rows * depth, 12 * depth * rows),
        name="last_part",
    )(got, powers, mix, scales, prior_t)


def exchanged(x):
    return lax.all_to_all(x, "member", split_axis=0, concat_axis=0, tiled=True)


def body(embeddings, prior, source_member, source_block, cross_block, row_links):
    relays = lax.axis_size("member")
    groups = lax.axis_size("group")
    group = lax.axis_index("group")
    rows = embeddings.shape[0]
    owners, blocks = source_member[0], source_block[0]
    near_slots = owners.shape[1]
    prior_t, links_t = prior.T, row_links.T
    up = [(i, (i + 1) % groups) for i in range(groups)]
    down = [(j, i) for i, j in up]
    asked = cross_block[:, 0, :]
    to_above = lax.dynamic_slice(asked, ((group + 1) % groups, 0), (1, 1)).reshape(1)
    to_below = lax.dynamic_slice(asked, ((group + groups - 1) % groups, 1), (1, 1)).reshape(1)

    spread = prep(prior_t, embeddings, relays)
    relayed = exchanged(spread)
    below = lax.ppermute(pack(to_above, embeddings, spread), "group", up)
    above = lax.ppermute(pack(to_below, embeddings, spread), "group", down)
    far_powers, mix, stat, turned = own_part(embeddings, spread, below, above, links_t, prior_t, near_slots)
    near = exchanged(select(owners, blocks, relayed, stat))
    labels_t, near_powers, scales = near_part(near, turned, links_t, mix, stat, prior_t)

    relayed = exchanged(labels_t.reshape(relays, SUB, rows))
    below = lax.ppermute(pack_labels(to_above, labels_t), "group", up)
    above = lax.ppermute(pack_labels(to_below, labels_t), "group", down)
    mix = remix(labels_t, below, above, far_powers)
    near = exchanged(select(owners, blocks, relayed, mix))
    return last_part(near, near_powers, mix, scales, prior_t).T


def solution(mesh):
    placed = (
        P(("group", "member"), None),
        P(("group", "member"), None),
        P("group", None, None),
        P("group", None, None),
        P(None, "member", None),
        P(("group", "member"), None),
    )
    return jax.shard_map(
        body, mesh=mesh, in_specs=placed, out_specs=P(("group", "member"), None), check_vma=False
    )
```

```python
import jax
import jax.numpy as jnp
from jax import lax
from jax.experimental import pallas as pl
from jax.experimental.pallas import tpu as pltpu
from jax.sharding import PartitionSpec as P

BR = 128
MIXING = 0.8
SUB = 32
QB = 256
PARTS = 5
STORES = 4
GROUP = 2
BF = jnp.bfloat16
F32 = jnp.float32
VMEM_BYTES = 24 * 1024 * 1024


def params():
    return pltpu.CompilerParams(
        dimension_semantics=("arbitrary",), vmem_limit_bytes=VMEM_BYTES
    )


def in_hbm(x):
    return pltpu.with_memory_space_constraint(x, pltpu.HBM)


def cost(flops, size, exps=0):
    return pl.CostEstimate(flops=flops, bytes_accessed=size, transcendentals=exps)


def nn(a, b):
    return jnp.dot(a, b, preferred_element_type=F32)


def padded(x, rows):
    if x.shape[0] == rows:
        return x
    return jnp.concatenate([x, jnp.zeros((rows - x.shape[0], x.shape[1]), x.dtype)], axis=0)


def prep_kernel(prior_ref, emb_ref, out_ref, prior_buf, emb_buf, out_buf, sem_p, sem_e, sem_o):
    relays, _, rows = out_ref.shape
    classes, features = prior_ref.shape[0], emb_ref.shape[1]
    wide, tall = features // BR, BR // SUB
    part = classes // PARTS
    loads = [
        pltpu.make_async_copy(
            prior_ref.at[pl.ds(i * part, part)], prior_buf.at[pl.ds(i * part, part)], sem_p.at[i]
        )
        for i in range(PARTS)
    ]
    pieces = [
        pltpu.make_async_copy(emb_ref.at[pl.ds(b * BR, BR)], emb_buf.at[pl.ds(b * BR, BR)], sem_e.at[b])
        for b in range(rows // BR)
    ]
    for copy in (*pieces, *loads):
        copy.start()
    for b, copy in enumerate(pieces):
        copy.wait()
        for r in range(tall):
            at = b * BR + r * SUB
            for f in range(wide):
                out_buf[r * wide + f, SUB:, b * BR : (b + 1) * BR] = emb_buf[
                    at : at + SUB, f * BR : (f + 1) * BR
                ]
    stores = [
        pltpu.make_async_copy(
            out_buf.at[:, pl.ds(SUB, SUB)], out_ref.at[:, pl.ds(SUB, SUB)], sem_o.at[STORES]
        )
    ]
    stores[0].start()
    total = jnp.zeros((8, rows), F32)
    for i, copy in enumerate(loads):
        copy.wait()
        rest = prior_buf[i * part : (i + 1) * part].reshape(part // 8, 8, rows)
        total = total + jnp.sum(rest, axis=0)
    inverse = 1.0 / jnp.sum(total, axis=0, keepdims=True)
    batch = relays // STORES
    for i in range(STORES):
        for m in range(i * batch, (i + 1) * batch):
            end = min(classes, (m + 1) * SUB)
            share = padded(prior_buf[m * SUB : end] * inverse, SUB)
            out_buf[m, :SUB, :] = share.astype(BF)
        stores.append(
            pltpu.make_async_copy(
                out_buf.at[pl.ds(i * batch, batch), pl.ds(0, SUB)],
                out_ref.at[pl.ds(i * batch, batch), pl.ds(0, SUB)],
                sem_o.at[i],
            )
        )
        stores[-1].start()
    for copy in stores:
        copy.wait()


def prep(prior_t, emb, relays):
    classes, rows = prior_t.shape
    features = emb.shape[1]
    shape = (relays, 2 * SUB, rows)
    return pl.pallas_call(
        prep_kernel,
        in_specs=[pl.BlockSpec(memory_space=pl.ANY)] * 2,
        out_specs=pl.BlockSpec(memory_space=pl.ANY),
        out_shape=jax.ShapeDtypeStruct(shape, BF),
        scratch_shapes=[
            pltpu.VMEM((classes, rows), F32),
            pltpu.VMEM((rows, features), BF),
            pltpu.VMEM(shape, BF),
            pltpu.SemaphoreType.DMA((PARTS,)),
            pltpu.SemaphoreType.DMA((rows // BR,)),
            pltpu.SemaphoreType.DMA((STORES + 1,)),
        ],
        compiler_params=pltpu.CompilerParams(vmem_limit_bytes=VMEM_BYTES),
        cost_estimate=cost(4 * classes * rows, 4 * classes * rows + 4 * features * rows),
        name="prep",
    )(in_hbm(prior_t), in_hbm(emb))


def select_kernel(owner_ref, block_ref, got_ref, after_ref, out_ref):
    members, slots = owner_ref.shape

    @pl.loop(0, members, unroll=8)
    def _(d):
        for k in range(slots):
            lane = pl.multiple_of(block_ref[d, k] * BR, BR)
            out_ref[d, :, k * BR : (k + 1) * BR] = got_ref[owner_ref[d, k], :, pl.ds(lane, BR)]


def select(owners, blocks, got, after):
    members, slots = owners.shape
    depth = got.shape[1]
    return pl.pallas_call(
        select_kernel,
        in_specs=[
            pl.BlockSpec(memory_space=pltpu.SMEM),
            pl.BlockSpec(memory_space=pltpu.SMEM),
            pl.BlockSpec(memory_space=pltpu.VMEM),
            pl.BlockSpec(memory_space=pl.ANY),
        ],
        out_specs=pl.BlockSpec(memory_space=pltpu.VMEM),
        out_shape=jax.ShapeDtypeStruct((members, depth, slots * BR), BF),
        compiler_params=pltpu.CompilerParams(vmem_limit_bytes=VMEM_BYTES),
        cost_estimate=cost(0, 4 * got.size),
        name="select",
    )(owners, blocks, got, after)


def pack_kernel(pick_ref, emb_ref, lab_ref, out_ref):
    out_ref[:BR] = emb_ref[...]
    labels = lab_ref[...].reshape(-1, BR)
    for f in range(labels.shape[0] // BR):
        out_ref[BR:, f * BR : (f + 1) * BR] = labels[f * BR : (f + 1) * BR]


def pack(pick, emb, spread):
    relays = spread.shape[0]
    features = emb.shape[1]
    return pl.pallas_call(
        pack_kernel,
        grid_spec=pltpu.PrefetchScalarGridSpec(
            num_scalar_prefetch=1,
            grid=(1,),
            in_specs=[
                pl.BlockSpec((BR, features), lambda i, p: (p[0], 0)),
                pl.BlockSpec((relays, SUB, BR), lambda i, p: (0, 0, p[0])),
            ],
            out_specs=pl.BlockSpec((2 * BR, features), lambda i, p: (0, 0)),
        ),
        out_shape=jax.ShapeDtypeStruct((2 * BR, features), BF),
        compiler_params=params(),
        cost_estimate=cost(0, 8 * BR * features),
        name="pack_cross",
    )(pick, in_hbm(emb), spread)


def pack_labels_kernel(pick_ref, lab_ref, out_ref):
    out_ref[...] = lab_ref[...]


def pack_labels(pick, labels_t):
    depth = labels_t.shape[0]
    return pl.pallas_call(
        pack_labels_kernel,
        grid_spec=pltpu.PrefetchScalarGridSpec(
            num_scalar_prefetch=1,
            grid=(1,),
            in_specs=[pl.BlockSpec((depth, BR), lambda i, p: (0, p[0]))],
            out_specs=pl.BlockSpec((depth, BR), lambda i, p: (0, 0)),
        ),
        out_shape=jax.ShapeDtypeStruct((depth, BR), BF),
        compiler_params=params(),
        cost_estimate=cost(0, 4 * BR * depth),
        name="pack_labels",
    )(pick, labels_t)


def slot_hit(links, slot):
    return jnp.max(jnp.where(links == slot, 1.0, 0.0), axis=0, keepdims=True) > 0.0


def own_kernel(near_slots, emb_ref, q_ref, lab_ref, below_ref, above_ref, links_ref, prior_ref, p_ref, mix_ref, stat_ref, turned_ref, far_ref):
    step = pl.program_id(0)
    rows, features = emb_ref.shape
    depth = mix_ref.shape[0]

    @pl.when(step == 0)
    def _():
        for f in range(depth // BR):
            for s, ref in enumerate((below_ref, above_ref)):
                far_ref[f * BR : (f + 1) * BR, s * BR : (s + 1) * BR] = ref[BR:, f * BR : (f + 1) * BR]

    q = q_ref[...].T
    turned_ref[...] = q
    scale = features ** (-0.5)
    own = nn(emb_ref[...], q) * scale
    key_id = lax.broadcasted_iota(jnp.int32, own.shape, 0)
    row_id = lax.broadcasted_iota(jnp.int32, own.shape, 1) + step * QB
    own = jnp.where(key_id == row_id, -jnp.inf, own)
    links = links_ref[...]
    parts = [own]
    for s, ref in enumerate((below_ref, above_ref)):
        far = nn(ref[:BR], q) * scale
        parts.append(jnp.where(slot_hit(links, near_slots + s), far, -jnp.inf))
    scores = jnp.concatenate(parts, axis=0)
    top = jnp.max(scores, axis=0, keepdims=True)
    powers = jnp.exp(scores - top)
    total = jnp.sum(powers, axis=0, keepdims=True)
    powers = powers.astype(BF)
    p_ref[...] = powers
    mix_ref[...] = nn(lab_ref[...].reshape(depth, rows), powers[:rows]) + nn(far_ref[...], powers[rows:])
    share = (1.0 - MIXING) / jnp.sum(prior_ref[...], axis=0, keepdims=True)
    stat_ref[...] = jnp.concatenate([top, total, share, jnp.zeros((5, QB), F32)], axis=0)


def own_part(emb, spread, below, above, links_t, prior_t, near_slots):
    rows, features = emb.shape
    relays = spread.shape[0]
    depth = relays * SUB
    keys = rows + 2 * BR
    return pl.pallas_call(
        lambda *refs: own_kernel(near_slots, *refs),
        grid=(rows // QB,),
        in_specs=[
            pl.BlockSpec((rows, features), lambda i: (0, 0)),
            pl.BlockSpec((QB, features), lambda i: (i, 0)),
            pl.BlockSpec((relays, SUB, rows), lambda i: (0, 0, 0)),
            pl.BlockSpec((2 * BR, features), lambda i: (0, 0)),
            pl.BlockSpec((2 * BR, features), lambda i: (0, 0)),
            pl.BlockSpec((links_t.shape[0], QB), lambda i: (0, i)),
            pl.BlockSpec((prior_t.shape[0], QB), lambda i: (0, i)),
        ],
        out_specs=[
            pl.BlockSpec((keys, QB), lambda i: (0, i)),
            pl.BlockSpec((depth, QB), lambda i: (0, i)),
            pl.BlockSpec((8, QB), lambda i: (0, i)),
            pl.BlockSpec((features, QB), lambda i: (0, i)),
        ],
        out_shape=[
            pltpu.HBM((keys, rows), BF),
            pltpu.HBM((depth, rows), F32),
            jax.ShapeDtypeStruct((8, rows), F32),
            pltpu.HBM((features, rows), BF),
        ],
        scratch_shapes=[pltpu.VMEM((depth, 2 * BR), BF)],
        compiler_params=params(),
        cost_estimate=cost(4 * keys * rows * features, 12 * depth * rows, keys * rows),
        name="own_part",
    )(in_hbm(emb), in_hbm(emb), spread, below, above, links_t, in_hbm(prior_t))


def near_kernel(
    got_ref, turned_ref, links_ref, mix_ref, stat_ref, prior_ref,
    lab_ref, p_ref, out_ref,
    key_ref, mixed_buf, lab_buf, p_buf, sem_l, sem_p,
):
    features, rows = turned_ref.shape
    relays = got_ref.shape[0]
    slots = got_ref.shape[2] // BR
    wide = features // BR
    for s in range(slots):
        for r in range(BR // SUB):
            at = s * BR + r * SUB
            for f in range(wide):
                key_ref[at : at + SUB, f * BR : (f + 1) * BR] = got_ref[
                    r * wide + f, SUB:, s * BR : (s + 1) * BR
                ]
    near_labels = got_ref[:, :SUB, :].reshape(relays * SUB, slots * BR)
    copies = []
    for i in range(rows // QB):
        at = slice(i * QB, (i + 1) * QB)
        links = links_ref[:, at]
        scores = nn(key_ref[...], turned_ref[:, at]) * features ** (-0.5)
        scores = jnp.concatenate(
            [
                jnp.where(slot_hit(links, s), scores[s * BR : (s + 1) * BR], -jnp.inf)
                for s in range(slots)
            ],
            axis=0,
        )
        own_top = stat_ref[0:1, at]
        top = jnp.maximum(own_top, jnp.max(scores, axis=0, keepdims=True))
        powers = jnp.exp(scores - top)
        lower = jnp.exp(own_top - top)
        total = lower * stat_ref[1:2, at] + jnp.sum(powers, axis=0, keepdims=True)
        inverse = MIXING / total
        lower = lower * inverse
        powers = powers.astype(BF)
        p_buf[i] = powers
        copies.append(pltpu.make_async_copy(p_buf.at[i], p_ref.at[:, pl.ds(i * QB, QB)], sem_p.at[i]))
        copies[-1].start()
        share = stat_ref[2:3, at]
        out_ref[:, at] = jnp.concatenate([lower, inverse, share, jnp.zeros((5, QB), F32)], axis=0)
        mixed_buf[i] = nn(near_labels, powers)
        norm = squares(mixed_buf.at[i], mix_ref, prior_ref, at, lower, inverse, share)
        for start, end in tiles(prior_ref.shape[0]):
            sharp = padded(mixed_buf[i, start:end] * norm, BR)
            lab_buf[i, start : start + BR] = sharp.astype(BF)
            if (start // BR) % GROUP == GROUP - 1:
                at_rows = pl.ds(start + BR - GROUP * BR, GROUP * BR)
                copies.append(
                    pltpu.make_async_copy(
                        lab_buf.at[i, at_rows],
                        lab_ref.at[at_rows, pl.ds(i * QB, QB)],
                        sem_l.at[i, start // (GROUP * BR)],
                    )
                )
                copies[-1].start()
    for copy in copies:
        copy.wait()


def tiles(classes):
    return [(start, min(start + BR, classes)) for start in range(0, classes, BR)]


def squares(buf, mix_ref, prior_ref, at, lower, inverse, share):
    total = jnp.zeros((8, QB), F32)
    for start, end in tiles(prior_ref.shape[0]):
        mixed = mix_ref[start:end, at] * lower + buf[start:end] * inverse + prior_ref[start:end, at] * share
        mixed = mixed * mixed
        buf[start:end] = mixed
        total = total + jnp.sum(mixed.reshape(-1, 8, QB), axis=0)
    return 1.0 / jnp.sum(total, axis=0, keepdims=True)


def near_part(got, turned, links_t, mix, stat, prior_t):
    features, rows = turned.shape
    relays, _, near_keys = got.shape
    depth, steps = relays * SUB, rows // QB
    whole = pl.BlockSpec(memory_space=pltpu.VMEM)
    return pl.pallas_call(
        near_kernel,
        in_specs=[whole] * 6,
        out_specs=[pl.BlockSpec(memory_space=pl.ANY)] * 2 + [whole],
        out_shape=[
            pltpu.HBM((depth, rows), BF),
            pltpu.HBM((near_keys, rows), BF),
            jax.ShapeDtypeStruct((8, rows), F32),
        ],
        scratch_shapes=[
            pltpu.VMEM((near_keys, features), BF),
            pltpu.VMEM((steps, depth, QB), F32),
            pltpu.VMEM((steps, depth, QB), BF),
            pltpu.VMEM((steps, near_keys, QB), BF),
            pltpu.SemaphoreType.DMA((steps, depth // (GROUP * BR))),
            pltpu.SemaphoreType.DMA((steps,)),
        ],
        compiler_params=pltpu.CompilerParams(vmem_limit_bytes=VMEM_BYTES),
        cost_estimate=cost(4 * near_keys * rows * features, 12 * depth * rows, near_keys * rows),
        name="near_part",
    )(got, turned, links_t, mix, stat, prior_t)


def remix_kernel(lab_ref, below_ref, above_ref, p_ref, out_ref):
    rows = lab_ref.shape[1]
    far = jnp.concatenate([below_ref[...], above_ref[...]], axis=1)
    out_ref[...] = nn(lab_ref[...], p_ref[:rows]) + nn(far, p_ref[rows:])


def remix(labels_t, below, above, powers):
    depth, rows = labels_t.shape
    keys = powers.shape[0]
    return pl.pallas_call(
        remix_kernel,
        grid=(rows // QB,),
        in_specs=[
            pl.BlockSpec((depth, rows), lambda i: (0, 0)),
            pl.BlockSpec((depth, BR), lambda i: (0, 0)),
            pl.BlockSpec((depth, BR), lambda i: (0, 0)),
            pl.BlockSpec((keys, QB), lambda i: (0, i)),
        ],
        out_specs=pl.BlockSpec((depth, QB), lambda i: (0, i)),
        out_shape=jax.ShapeDtypeStruct((depth, rows), F32),
        compiler_params=params(),
        cost_estimate=cost(2 * keys * rows * depth, 8 * depth * rows),
        name="remix",
    )(labels_t, below, above, powers)


def last_kernel(got_ref, p_ref, mix_ref, scale_ref, prior_ref, out_ref, mixed_buf, buf, sem):
    relays, sub, near_keys = got_ref.shape
    classes, rows = prior_ref.shape
    near_labels = got_ref[...].reshape(relays * sub, near_keys)
    copies = []
    for i in range(rows // QB):
        at = slice(i * QB, (i + 1) * QB)
        mixed_buf[i] = nn(near_labels, p_ref[:, at])
        scales = [scale_ref[k : k + 1, at] for k in range(3)]
        norm = squares(mixed_buf.at[i], mix_ref, prior_ref, at, *scales) * float(classes)
        for start, end in tiles(classes):
            buf[i, start:end] = mixed_buf[i, start:end] * norm
            if (start // BR) % GROUP == GROUP - 1 or end == classes:
                first = start // (GROUP * BR)
                at_rows = pl.ds(first * GROUP * BR, end - first * GROUP * BR)
                copies.append(
                    pltpu.make_async_copy(
                        buf.at[i, at_rows], out_ref.at[at_rows, pl.ds(i * QB, QB)], sem.at[i, first]
                    )
                )
                copies[-1].start()
    for copy in copies:
        copy.wait()


def last_part(got, powers, mix, scales, prior_t):
    relays, sub, near_keys = got.shape
    classes, rows = prior_t.shape
    depth, steps = relays * sub, rows // QB
    return pl.pallas_call(
        last_kernel,
        in_specs=[pl.BlockSpec(memory_space=pltpu.VMEM)] * 5,
        out_specs=pl.BlockSpec(memory_space=pl.ANY),
        out_shape=jax.ShapeDtypeStruct((classes, rows), F32),
        scratch_shapes=[
            pltpu.VMEM((steps, depth, QB), F32),
            pltpu.VMEM((steps, classes, QB), F32),
            pltpu.SemaphoreType.DMA((steps, depth // (GROUP * BR))),
        ],
        compiler_params=pltpu.CompilerParams(vmem_limit_bytes=VMEM_BYTES),
        cost_estimate=cost(2 * near_keys * rows * depth, 12 * depth * rows),
        name="last_part",
    )(got, powers, mix, scales, prior_t)


def exchanged(x):
    return lax.all_to_all(x, "member", split_axis=0, concat_axis=0, tiled=True)


def body(embeddings, prior, source_member, source_block, cross_block, row_links):
    relays = lax.axis_size("member")
    groups = lax.axis_size("group")
    group = lax.axis_index("group")
    rows = embeddings.shape[0]
    owners, blocks = source_member[0], source_block[0]
    near_slots = owners.shape[1]
    prior_t, links_t = prior.T, row_links.T
    up = [(i, (i + 1) % groups) for i in range(groups)]
    down = [(j, i) for i, j in up]
    asked = cross_block[:, 0, :]
    to_above = lax.dynamic_slice(asked, ((group + 1) % groups, 0), (1, 1)).reshape(1)
    to_below = lax.dynamic_slice(asked, ((group + groups - 1) % groups, 1), (1, 1)).reshape(1)

    spread = prep(prior_t, embeddings, relays)
    relayed = exchanged(spread)
    below = lax.ppermute(pack(to_above, embeddings, spread), "group", up)
    above = lax.ppermute(pack(to_below, embeddings, spread), "group", down)
    far_powers, mix, stat, turned = own_part(embeddings, spread, below, above, links_t, prior_t, near_slots)
    near = exchanged(select(owners, blocks, relayed, stat))
    labels_t, near_powers, scales = near_part(near, turned, links_t, mix, stat, prior_t)

    relayed = exchanged(labels_t.reshape(relays, SUB, rows))
    below = lax.ppermute(pack_labels(to_above, labels_t), "group", up)
    above = lax.ppermute(pack_labels(to_below, labels_t), "group", down)
    mix = remix(labels_t, below, above, far_powers)
    near = exchanged(select(owners, blocks, relayed, mix))
    return last_part(near, near_powers, mix, scales, prior_t).T


def solution(mesh):
    placed = (
        P(("group", "member"), None),
        P(("group", "member"), None),
        P("group", None, None),
        P("group", None, None),
        P(None, "member", None),
        P(("group", "member"), None),
    )
    return jax.shard_map(
        body, mesh=mesh, in_specs=placed, out_specs=P(("group", "member"), None), check_vma=False
    )
```
